128 devices in a mesh: rows: 32 (over y_hi, x, z), rep: 4 (over y_lo, core).
Axes of the slice: x: 4, y: 4 (y_hi: 2, y_lo: 2; y = y_hi * 2 + y_lo), z: 4, core: 2. Of those that a mesh axis runs over, the one named last changes fastest.
Arguments:
- features: bfloat16 [65536, 256], P('rows'), may hold values from -6 to 6
- weight: bfloat16 [256, 256], replicated, may hold values from -0.375 to 0.375
- bias: float32 [256], replicated, may hold values from -3 to 3
- cotangent: bfloat16 [65536, 256], P(('rows', 'rep')), may hold values from -6 to 6
- tile_vals: bfloat16 [32, 4, 32, 4, 128, 128], P('rows', 'rep'), may hold values from -0.09375 to 0.09375
- tile_rows: int32 [32, 4, 32, 4], P('rows', 'rep'), may hold values from 0 to 15
- tile_pick: int32 [32, 4, 32, 4], P('rows', 'rep'), may hold values from 0 to 1
- tile_count: int32 [32, 4, 32], P('rows', 'rep'), may hold values from 0 to 4, as said below
- pull_cols: int32 [32, 4, 32, 2], P('rows', 'rep'), may hold values from 0 to 3
Outputs:
- activations: bfloat16 [65536, 256], P(('rows', 'rep'))
- feature_grads: float32 [65536, 256], P(('rows', 'rep'))
- weight_grad: float32 [256, 256], replicated
- bias_grad: float32 [256], replicated
The draws below stay inside these ranges and needn't reach their ends.
Inputs may be any that keep to these rules, and one draw needn't show every extreme that they name: Only the first tile_count slots of a row block, column quarter and section are live; the others are padding. Some entry equals 4 in every draw.
All inputs are finite; a program needn't handle non-finite values.
Results may differ from the reference program's by a relative error of at most 0.0052.
Values may be sent and summed in bfloat16 or wider, within the bound.
A program may use at most 128 MiB of HBM per device.

```python
import jax
import jax.numpy as jnp
from jax import lax

FIN = 256
FOUT = 256
NODE_DEV = 2048
TILE = 128
TPS = 4
PULL = 2
NODES = 65536
ROW_TILES = 16
COL_TILES = 4
TILE_FAN = 4096
N_ROWS = 32
N_REP = 4


def draw_tile_count(key, part):
    key = jax.random.fold_in(key, 7)
    key_load, key_base, key_spot = jax.random.split(key, 3)
    half = TPS // 2
    heavy = (jax.random.randint(key_load, (N_ROWS, 1, 1), 0, 4) == 0).astype(jnp.int32)
    base = jax.random.randint(key_base, (N_ROWS, N_REP, N_ROWS), 0, half + 1)
    counts = jnp.maximum(base, heavy * TPS)
    spot = jax.random.randint(key_spot, (), 0, N_ROWS * N_REP * N_ROWS)
    flat = counts.reshape(-1)
    flat = jnp.where(jnp.arange(flat.shape[0]) == spot, TPS, flat)
    return flat.reshape(N_ROWS, N_REP, N_ROWS).astype(jnp.int32)


def with_ends(values, own_key, low, top_value):
    place = [jax.random.randint(jax.random.fold_in(own_key, axis), (), 0, length) for axis, length in enumerate(values.shape)]
    longest = values.shape.index(max(values.shape))
    next_to = place[:longest] + [(place[longest] + 1) % values.shape[longest]] + place[longest + 1:]
    return values.at[tuple(place)].set(low).at[tuple(next_to)].set(top_value)


def steps_of(key, extent, pieces, least, largest):
    def one(position, blocks):
        draws = jax.random.uniform(jax.random.fold_in(jax.random.fold_in(key, 6), position), (blocks,), jnp.float32, least / len(pieces), largest / len(pieces))
        return jnp.repeat(jnp.exp(draws), extent[position] // blocks).reshape((-1,) + (1,) * (len(extent) - position - 1))

    loudness = one(*pieces[0])
    for cut in pieces[1:]:
        loudness = loudness * one(*cut)
    return loudness


def normal_values(stream_key, shape, spread, bound, cuts=(), dtype=jnp.bfloat16):
    entries = spread * jax.random.normal(stream_key, shape, jnp.float32)
    if cuts:
        entries = entries * steps_of(stream_key, shape, cuts, -0.22, 0.18)
    return jnp.clip(entries, -bound, bound).astype(dtype)


def setup_inputs(seed: int = 0) -> dict:
    streams_of = jax.random.split(jax.random.key(seed), 10)
    return {
        "features": normal_values(streams_of[0], (NODES, FIN), 1.0, 6.0, ((0, 32),)),
        "weight": normal_values(streams_of[1], (FIN, FOUT), FIN ** -0.5, 0.375),
        "bias": normal_values(streams_of[2], (FOUT,), 0.5, 3.0, (), jnp.float32),
        "cotangent": normal_values(streams_of[3], (NODES, FOUT), 1.0, 6.0, ((0, 128),)),
        "tile_vals": normal_values(streams_of[4], (N_ROWS, N_REP, N_ROWS, TPS, TILE, TILE), TILE_FAN ** -0.5, 0.09375, ((0, 32), (1, 4))),
        "tile_rows": with_ends(jax.random.randint(streams_of[5], (N_ROWS, N_REP, N_ROWS, TPS), 0, ROW_TILES), jax.random.fold_in(streams_of[5], 1), 0, ROW_TILES - 1).astype(jnp.int32),
        "tile_pick": with_ends(jax.random.randint(streams_of[6], (N_ROWS, N_REP, N_ROWS, TPS), 0, PULL), jax.random.fold_in(streams_of[6], 1), 0, PULL - 1).astype(jnp.int32),
        "tile_count": draw_tile_count(jax.random.fold_in(streams_of[9], 71), 0),
        "pull_cols": with_ends(jax.random.randint(streams_of[8], (N_ROWS, N_REP, N_ROWS, PULL), 0, COL_TILES), jax.random.fold_in(streams_of[8], 1), 0, COL_TILES - 1).astype(jnp.int32),
    }


def silu_slope(pre):
    sig = jax.nn.sigmoid(pre)
    return sig * (1.0 + pre * (1.0 - sig))


def reference(features, weight, bias, cotangent, tile_vals, tile_rows, tile_pick, tile_count, pull_cols):
    quarter = NODE_DEV // N_REP
    col_tiles = quarter // TILE
    row_tiles = NODE_DEV // TILE
    blocks = features.reshape(N_ROWS, N_REP, col_tiles, TILE, FIN)
    live = (jnp.arange(TPS)[None, None, None, :] < tile_count[..., None]).astype(jnp.float32)
    col_ids = jnp.take_along_axis(pull_cols, tile_pick, axis=3)
    section_idx = jnp.arange(N_ROWS)[None, :, None]
    rep_idx = jnp.arange(N_REP)[:, None, None]

    def forward_block(block):
        values = tile_vals[block].astype(jnp.float32)
        sources = blocks[section_idx, rep_idx, col_ids[block]].astype(jnp.float32)
        prods = jnp.einsum("rctab,rctbf->rctaf", values, sources) * live[block][..., None, None]
        return jnp.zeros((row_tiles, TILE, FIN), jnp.float32).at[tile_rows[block]].add(prods)

    total = lax.map(forward_block, jnp.arange(N_ROWS)).reshape(N_ROWS * NODE_DEV, FIN)
    aggregated = total.astype(jnp.bfloat16)
    pre = jnp.dot(aggregated, weight, preferred_element_type=jnp.float32) + bias
    activations = jax.nn.silu(pre).astype(jnp.bfloat16)
    slope = (cotangent.astype(jnp.float32) * silu_slope(pre)).astype(jnp.bfloat16)
    weight_grad = jnp.dot(aggregated.T, slope, preferred_element_type=jnp.float32)
    bias_grad = jnp.sum(slope.astype(jnp.float32), axis=0)
    back = lax.dot_general(slope, weight, (((1,), (1,)), ((), ())), preferred_element_type=jnp.float32).astype(jnp.bfloat16)
    back_blocks = back.reshape(N_ROWS, row_tiles, TILE, FIN)

    def backward_block(accum, block):
        values = tile_vals[block].astype(jnp.float32)
        sources = back_blocks[block][tile_rows[block]].astype(jnp.float32)
        terms = jnp.einsum("rctba,rctbf->rctaf", values, sources) * live[block][..., None, None]
        return accum.at[section_idx, rep_idx, col_ids[block]].add(terms), None

    start_acc = jnp.zeros((N_ROWS, N_REP, col_tiles, TILE, FIN), jnp.float32)
    accum, unused = lax.scan(backward_block, start_acc, jnp.arange(N_ROWS))
    feature_grads = accum.reshape(N_ROWS * NODE_DEV, FIN)
    return (activations, feature_grads, weight_grad, bias_grad)
```

```python
import functools

import jax
import jax.numpy as jnp
from jax import lax
from jax.experimental import pallas as pl
from jax.experimental.pallas import tpu as pltpu
from jax.sharding import PartitionSpec as P

MESH = pl.DeviceIdType.MESH
BF = jnp.bfloat16
F32 = jnp.float32
TILE = 128
WIDTH = 256
SECTIONS = 32
SLOTS = 4
QUARTER = 512
ROWS = 2048
VMEM_LIMIT = 50 << 20


class Place:
    def __init__(self):
        rows, rep = lax.axis_index("rows"), lax.axis_index("rep")
        self.yh, x, z = rows // 16, (rows // 4) % 4, rows % 4
        self.yl, self.core = rep // 2, rep % 2
        self.a = x + self.core * (z - x)
        self.b = z + self.core * (x - z)

    def section(self, yh, a, b):
        x = a + self.core * (b - a)
        z = b + self.core * (a - b)
        return yh * 16 + x * 4 + z

    def a_peer(self, j):
        return (self.section(self.yh, (self.a + j) % 4, self.b), self.yl * 2 + self.core)

    def b_peer(self, j):
        return (self.section(self.yh, self.a, (self.b + j) % 4), self.yl * 2 + self.core)

    def y_peer(self):
        return (self.section(1 - self.yh, self.a, self.b), self.yl * 2 + self.core)

    def near_peer(self, mask):
        yh = (self.yh + mask // 4) % 2
        yl = (self.yl + (mask // 2) % 2) % 2
        core = (self.core + mask % 2) % 2
        rows, _ = lax.axis_index("rows"), None
        return (yh * 16 + rows % 16, yl * 2 + core)

    def near_id(self):
        return self.yh * 4 + self.yl * 2 + self.core

    def chunk(self, b, a):
        return b * 4 + a + self.core * (a * 4 + b - b * 4 - a)


def greet(peers):
    barrier = pltpu.get_barrier_semaphore()
    for peer in peers:
        pl.semaphore_signal(barrier, inc=1, device_id=peer, device_id_type=MESH)
    pl.semaphore_wait(barrier, len(peers))


def remote(src, dst, send, recv, peer):
    return pltpu.make_async_remote_copy(
        src_ref=src, dst_ref=dst, send_sem=send, recv_sem=recv, device_id=peer, device_id_type=MESH
    )


def pull_kernel(
    features, pull_vec, pull_own, out, asked, *scratch
):
    dense, scratch = scratch[:8], scratch[8:]
    (packed, wants, own_sem, want_sem, ask_send, ask_recv,
     y_send, y_recv, a_send, a_recv, b_send, b_recv) = scratch
    me = Place()
    fetch = pltpu.make_async_copy(
        features.at[pl.ds((me.yl * 2 + me.core) * 4, 4)], dense[0], own_sem
    )
    fetch.start()
    greet([me.y_peer()] + [me.a_peer(j) for j in (1, 2, 3)] + [me.b_peer(j) for j in (1, 2, 3)])

    def ask(j):
        return remote(pull_vec, asked.at[j - 1], ask_send.at[j - 1], ask_recv.at[j - 1], me.b_peer(j))

    for j in (1, 2, 3):
        ask(j).start()
    fetch.wait()

    across = remote(dense[0], dense[4], y_send, y_recv, me.y_peer())

    def along(h, j):
        return remote(
            dense[4 * h], dense[4 * h + j], a_send.at[h, j - 1], a_recv.at[h, j - 1], me.a_peer(j)
        )

    def place(h, j):
        return (me.yh + h) % 2, (me.a + 4 - j) % 4

    def give(h, j, to):
        yh, a = place(h, j)
        n = 4 * h + j
        return remote(
            packed.at[to - 1, n], out.at[me.b * 8 + yh * 4 + a],
            b_send.at[to - 1, n], b_recv.at[to - 1, n], me.b_peer(to),
        )

    across.start()
    for j in (1, 3, 2):
        along(0, j).start()
    for j in (1, 2, 3):
        ask(j).wait()
        table = pltpu.make_async_copy(asked.at[j - 1], wants.at[j - 1], want_sem)
        table.start()
        table.wait()

    def serve(h, j):
        column = me.section(*place(h, j), me.b)
        for source in (1, 3, 2):
            to = 4 - source
            for p in range(2):
                packed[to - 1, 4 * h + j, p] = dense[4 * h + j][wants[source - 1, column, p]]
            give(h, j, to).start()

    serve(0, 0)
    across.wait()
    for j in (1, 3, 2):
        along(1, j).start()
    serve(1, 0)
    for h in range(2):
        for j in (1, 3, 2):
            along(h, j).wait_recv()
            serve(h, j)
    for h in range(2):
        for j in range(4):
            yh, a = place(h, j)
            column = me.section(yh, a, me.b)
            for p in range(2):
                out[me.b * 8 + yh * 4 + a, p] = dense[4 * h + j][pull_own[column, p]]
    for h in range(2):
        for j in (1, 2, 3):
            along(h, j).wait_send()
    for to in (1, 2, 3):
        for h in range(2):
            for j in range(4):
                give(h, j, to).wait()


def pull(features, pull_cols):
    dma = pltpu.SemaphoreType.DMA
    vmem = pl.BlockSpec(memory_space=pltpu.VMEM)
    return pl.pallas_call(
        pull_kernel,
        name="pull",
        out_shape=(
            jax.ShapeDtypeStruct((SECTIONS, 2, TILE, WIDTH), BF),
            jax.ShapeDtypeStruct((3, SECTIONS, 2), jnp.int32),
        ),
        in_specs=[pl.BlockSpec(memory_space=pl.ANY), vmem, pl.BlockSpec(memory_space=pltpu.SMEM)],
        out_specs=(vmem, vmem),
        scratch_shapes=[
            *[pltpu.VMEM((4, TILE, WIDTH), BF)] * 8,
            pltpu.VMEM((3, 8, 2, TILE, WIDTH), BF),
            pltpu.SMEM((3, SECTIONS, 2), jnp.int32),
            dma, dma, dma((3,)), dma((3,)),
            dma, dma, dma((2, 3)), dma((2, 3)), dma((3, 8)), dma((3, 8)),
        ],
        compiler_params=pltpu.CompilerParams(
            collective_id=1, has_side_effects=True, vmem_limit_bytes=VMEM_LIMIT
        ),
    )(features.reshape(16, TILE, WIDTH), pull_cols, pull_cols)


def masked(values, section, picks, counts):
    halves = []
    for p in range(2):
        parts = []
        for t in range(SLOTS):
            keep = jnp.logical_and(picks[section, t] == p, t < counts[0, section])
            scale = jnp.where(keep, jnp.float32(1), jnp.float32(0))
            parts.append(values[section, t] * jnp.full((TILE, TILE), scale, F32).astype(BF))
        halves.append(jnp.concatenate(parts, axis=0))
    return jnp.concatenate(halves, axis=1)


def forward_kernel(values, pulled, rows, picks, counts, total):
    me = Place()
    total[...] = jnp.zeros_like(total)

    def one(place, carry):
        section = me.section((place // 4) % 2, place % 4, place // 8)
        block = pulled[place].reshape(2 * TILE, WIDTH)
        terms = jnp.dot(masked(values, section, picks, counts), block, preferred_element_type=F32)
        for t in range(SLOTS):
            total[rows[section, t]] += terms[t * TILE:(t + 1) * TILE]
        return carry

    lax.fori_loop(0, SECTIONS, one, 0, unroll=2)


def forward(values, pulled, rows, picks, counts):
    vmem, smem = pl.BlockSpec(memory_space=pltpu.VMEM), pl.BlockSpec(memory_space=pltpu.SMEM)
    return pl.pallas_call(
        forward_kernel,
        name="forward",
        out_shape=jax.ShapeDtypeStruct((16, TILE, WIDTH), F32),
        in_specs=[vmem, vmem, smem, smem, smem],
        out_specs=vmem,
        compiler_params=pltpu.CompilerParams(vmem_limit_bytes=VMEM_LIMIT),
    )(values, pulled, rows, picks, counts)


def dense_kernel(
    part, weight, bias, cotangent, act, back, wpart,
    from_core, to_y, from_y, core_send, core_recv, y_send, y_recv,
    g_core_send, g_core_recv, g_y_send, g_y_recv, f_send, f_recv,
):
    me = Place()
    core_peer, y_peer = me.near_peer(1), me.near_peer(2)
    greet([core_peer, y_peer])
    quarters = [(1 - me.yl) * 2, me.yl * 2]

    def swap(n, t):
        src = part.at[(quarters[n] + 1 - me.core) * 4 + t]
        return remote(src, from_core.at[n, t], core_send.at[n, t], core_recv.at[n, t], core_peer)

    def over(t):
        return remote(to_y.at[t], from_y.at[t], y_send.at[t], y_recv.at[t], y_peer)

    for n in range(2):
        for t in range(4):
            swap(n, t).start()
    for t in range(4):
        swap(0, t).wait_recv()
        to_y[t] = (part[(quarters[0] + me.core) * 4 + t] + from_core[0, t]).astype(BF)
        over(t).start()

    mine = me.yl * 2 + me.core
    yours = (1 - me.yl) * 2 + me.core

    def share_core(t):
        ref = back.at[mine * 4 + t]
        return remote(ref, ref, g_core_send.at[t], g_core_recv.at[t], core_peer)

    def share_y(t):
        ref = back.at[mine * 4 + t]
        return remote(ref, ref, g_y_send.at[t], g_y_recv.at[t], y_peer)

    def forward_on(t):
        ref = back.at[yours * 4 + t]
        return remote(ref, ref, f_send.at[t], f_recv.at[t], core_peer)

    grad = jnp.zeros((WIDTH, WIDTH), F32)
    bias_sum = jnp.zeros((1, WIDTH), F32)
    for t in range(4):
        swap(1, t).wait_recv()
        over(t).wait_recv()
        agg = (part[mine * 4 + t] + from_core[1, t] + from_y[t].astype(F32)).astype(BF)
        pre = jnp.dot(agg, weight[...], preferred_element_type=F32) + bias[...]
        sig = 1.0 / (1.0 + jnp.exp(-pre))
        act[t] = (pre * sig).astype(BF)
        slope = (cotangent[t].astype(F32) * (sig * (1.0 + pre * (1.0 - sig)))).astype(BF)
        back[mine * 4 + t] = lax.dot_general(
            slope, weight[...], (((1,), (1,)), ((), ())), preferred_element_type=F32
        ).astype(BF)
        share_y(t).start()
        share_core(t).start()
        grad += lax.dot_general(agg, slope, (((0,), (0,)), ((), ())), preferred_element_type=F32)
        bias_sum += jnp.sum(slope.astype(F32), axis=0, keepdims=True)

    for t in range(4):
        share_y(t).wait_recv()
        forward_on(t).start()
    wpart[:, 16:24, :] = jnp.zeros((16, 8, WIDTH), F32)
    wpart[0, 16:17, :] = bias_sum
    wpart[:, :16, :] = grad.reshape(16, 16, WIDTH)
    for t in range(4):
        share_y(t).wait_send()
        share_core(t).wait()
        forward_on(t).wait()
        over(t).wait_send()
        for n in range(2):
            swap(n, t).wait_send()


def dense_layer(part, weight, bias, cotangent):
    dma = pltpu.SemaphoreType.DMA
    vmem = pl.BlockSpec(memory_space=pltpu.VMEM)
    return pl.pallas_call(
        dense_kernel,
        name="dense",
        out_shape=(
            jax.ShapeDtypeStruct((4, TILE, WIDTH), BF),
            jax.ShapeDtypeStruct((16, TILE, WIDTH), BF),
            jax.ShapeDtypeStruct((16, 24, WIDTH), F32),
        ),
        in_specs=[vmem] * 4,
        out_specs=(vmem,) * 3,
        scratch_shapes=[
            pltpu.VMEM((2, 4, TILE, WIDTH), F32),
            pltpu.VMEM((4, TILE, WIDTH), BF),
            pltpu.VMEM((4, TILE, WIDTH), BF),
            dma((2, 4)), dma((2, 4)), dma((4,)), dma((4,)),
            dma((4,)), dma((4,)), dma((4,)), dma((4,)), dma((4,)), dma((4,)),
        ],
        compiler_params=pltpu.CompilerParams(
            collective_id=2, has_side_effects=True, vmem_limit_bytes=VMEM_LIMIT
        ),
    )(part, weight, bias.reshape(1, WIDTH), cotangent.reshape(4, TILE, WIDTH))


def push_kernel(
    values, back, wpart, rows, picks, counts, pulls, asked,
    fgrad, wgrad, bgrad,
    terms, from_b, to_a, from_a, held, to_y, from_y,
    w0, w1, s1, w2, s2, w3, s4, w5,
    b_send, b_recv, a_send, a_recv, y_send, y_recv,
    w1_send, w1_recv, w2_send, w2_recv, w3_send, w3_recv, w4_send, w4_recv, w5_send, w5_recv,
):
    me = Place()
    greet(
        [me.near_peer(m) for m in range(1, 8)]
        + [me.a_peer(j) for j in (1, 2, 3)]
        + [me.b_peer(j) for j in (1, 2, 3)]
    )

    for b in range(4):
        for a in range(4):
            w0[b, a] = wpart[me.chunk(b, a)]

    def w1_copy(j):
        return remote(w0.at[(me.b + j) % 4], w1.at[j - 1], w1_send.at[j - 1], w1_recv.at[j - 1], me.b_peer(j))

    for j in (1, 2, 3):
        w1_copy(j).start()

    def place(k):
        return (me.yh + 1 + k) % 2, (me.a + 1 + k // 2) % 4

    def give(k, j):
        return remote(
            terms.at[j, k], from_b.at[j - 1, k], b_send.at[j - 1, k], b_recv.at[j - 1, k], me.b_peer(j)
        )

    def products(k, j):
        yh, a = place(k)
        section = me.section(yh, a, (me.b + j) % 4)
        sources = jnp.concatenate([back[rows[section, t]] for t in range(SLOTS)], axis=0)
        terms[j, k] = lax.dot_general(
            masked(values, section, picks, counts), sources, (((0,), (0,)), ((), ())),
            preferred_element_type=F32,
        ).astype(BF)

    def send_off(step, carry):
        k, j = step // 3, 1 + step % 3
        products(k, j)
        give(k, j).start()
        return carry

    lax.fori_loop(0, 24, send_off, 0)

    def keep(k, carry):
        products(k, 0)
        return carry

    lax.fori_loop(0, 8, keep, 0)

    def w2_copy(j):
        return remote(s1.at[(me.a + j) % 4], w2.at[j - 1], w2_send.at[j - 1], w2_recv.at[j - 1], me.a_peer(j))

    def w3_copy(m):
        return remote(s2, w3.at[me.near_id()], w3_send.at[m - 1], w3_recv.at[m - 1], me.near_peer(m))

    def w4_copy(j):
        return remote(s4.at[me.a], s4.at[me.a], w4_send.at[j - 1], w4_recv.at[j - 1], me.a_peer(j))

    def w5_copy(j):
        return remote(s4, w5.at[me.b], w5_send.at[j - 1], w5_recv.at[j - 1], me.b_peer(j))

    for j in (1, 2, 3):
        w1_copy(j).wait()
    s1[...] = w0[me.b] + w1[0] + w1[1] + w1[2]
    for j in (1, 2, 3):
        w2_copy(j).start()
    for j in (1, 2, 3):
        w2_copy(j).wait()
    s2[...] = s1[me.a] + w2[0] + w2[1] + w2[2]
    for m in range(1, 8):
        w3_copy(m).start()
    w3[me.near_id()] = s2[...]
    for m in range(1, 8):
        w3_copy(m).wait()
    total = w3[0]
    for m in range(1, 8):
        total = total + w3[m]
    s4[me.a] = total
    for j in (1, 2, 3):
        w4_copy(j).start()

    def along(k):
        j = 1 + k // 2
        return remote(to_a.at[k], from_a.at[k], a_send.at[k], a_recv.at[k], me.a_peer(j))

    def gather_b(k, q):
        yh, a = place(k)
        section = me.section(yh, a, me.b)
        sums = jnp.zeros((TILE, WIDTH), F32)
        for source in range(4):
            for p in range(2):
                if source == 0:
                    hit, tile = pulls[section, p] == q, terms[0, k, p * TILE:(p + 1) * TILE]
                else:
                    hit = asked[source - 1, section, p] == q
                    tile = from_b[source - 1, k, p * TILE:(p + 1) * TILE]
                sums += tile.astype(F32) * jnp.where(hit, jnp.float32(1), jnp.float32(0))
        return sums

    def first(k, carry):
        for j in (1, 2, 3):
            give(k, j).wait_recv()

        def column(q, inner):
            to_a[k, q] = gather_b(k, q).astype(BF)
            return inner

        lax.fori_loop(0, 4, column, 0)
        along(k).start()
        return carry

    lax.fori_loop(0, 6, first, 0)
    for k in (6, 7):
        for j in (1, 2, 3):
            give(k, j).wait_recv()

        def column(q, inner):
            held[k - 6, q] = gather_b(k, q)
            return inner

        lax.fori_loop(0, 4, column, 0)

    for j in (1, 2, 3):
        w4_copy(j).wait()
    for j in (1, 2, 3):
        w5_copy(j).start()
    w5[me.b] = s4[...]

    across = remote(to_y, from_y, y_send, y_recv, me.y_peer())
    for j in range(3):
        along(2 * j).wait_recv()
    for q in range(4):
        to_y[q] = (
            held[0, q] + from_a[0, q].astype(F32) + from_a[2, q].astype(F32) + from_a[4, q].astype(F32)
        ).astype(BF)
    across.start()
    for j in range(3):
        along(2 * j + 1).wait_recv()
    for q in range(4):
        held[1, q] = (
            held[1, q] + from_a[1, q].astype(F32) + from_a[3, q].astype(F32) + from_a[5, q].astype(F32)
        )
    for j in (1, 2, 3):
        w5_copy(j).wait()
    for b in range(4):
        for a in range(4):
            wgrad[me.chunk(b, a)] = w5[b, a, :16]
    bgrad[...] = w5[0, 0, 16:17]
    across.wait()
    for q in range(4):
        fgrad[q] = held[1, q] + from_y[q].astype(F32)

    def drain(step, carry):
        give(step // 3, 1 + step % 3).wait_send()
        return carry

    lax.fori_loop(0, 24, drain, 0)
    for k in range(6):
        along(k).wait_send()


def push(values, back, wpart, rows, picks, counts, pulls, asked):
    dma = pltpu.SemaphoreType.DMA
    vmem, smem = pl.BlockSpec(memory_space=pltpu.VMEM), pl.BlockSpec(memory_space=pltpu.SMEM)
    return pl.pallas_call(
        push_kernel,
        name="push",
        out_shape=(
            jax.ShapeDtypeStruct((4, TILE, WIDTH), F32),
            jax.ShapeDtypeStruct((16, 16, WIDTH), F32),
            jax.ShapeDtypeStruct((1, WIDTH), F32),
        ),
        in_specs=[vmem, vmem, vmem, smem, smem, smem, smem, smem],
        out_specs=(vmem,) * 3,
        scratch_shapes=[
            pltpu.VMEM((4, 8, 2 * TILE, WIDTH), BF),
            pltpu.VMEM((3, 8, 2 * TILE, WIDTH), BF),
            pltpu.VMEM((6, 4, TILE, WIDTH), BF),
            pltpu.VMEM((6, 4, TILE, WIDTH), BF),
            pltpu.VMEM((2, 4, TILE, WIDTH), F32),
            pltpu.VMEM((4, TILE, WIDTH), BF),
            pltpu.VMEM((4, TILE, WIDTH), BF),
            pltpu.VMEM((4, 4, 24, WIDTH), F32),
            pltpu.VMEM((3, 4, 24, WIDTH), F32),
            pltpu.VMEM((4, 24, WIDTH), F32),
            pltpu.VMEM((3, 24, WIDTH), F32),
            pltpu.VMEM((24, WIDTH), F32),
            pltpu.VMEM((8, 24, WIDTH), F32),
            pltpu.VMEM((4, 24, WIDTH), F32),
            pltpu.VMEM((4, 4, 24, WIDTH), F32),
            dma((3, 8)), dma((3, 8)), dma((6,)), dma((6,)), dma, dma,
            dma((3,)), dma((3,)), dma((3,)), dma((3,)), dma((7,)), dma((7,)),
            dma((3,)), dma((3,)), dma((3,)), dma((3,)),
        ],
        compiler_params=pltpu.CompilerParams(
            collective_id=3, has_side_effects=True, vmem_limit_bytes=VMEM_LIMIT
        ),
    )(values, back, wpart, rows, picks, counts, pulls, asked)


def local(
    features, weight, bias, cotangent, tile_vals, tile_rows, tile_pick, tile_count, pull_cols
):
    values = tile_vals.reshape(SECTIONS, SLOTS, TILE, TILE)
    rows = tile_rows.reshape(SECTIONS, SLOTS)
    picks = tile_pick.reshape(SECTIONS, SLOTS)
    counts = tile_count.reshape(1, SECTIONS)
    pulls = pull_cols.reshape(SECTIONS, 2)
    pulled, asked = pull(features, pulls)
    part = forward(values, pulled, rows, picks, counts)
    act, back, wpart = dense_layer(part, weight, bias, cotangent)
    fgrad, wgrad, bgrad = push(values, back, wpart, rows, picks, counts, pulls, asked)
    return (
        act.reshape(QUARTER, WIDTH),
        fgrad.reshape(QUARTER, WIDTH),
        wgrad.reshape(WIDTH, WIDTH),
        bgrad.reshape(WIDTH),
    )


def solution(mesh):
    in_specs = (
        P("rows", None),
        P(),
        P(),
        P(("rows", "rep"), None),
        P("rows", "rep", None, None, None, None),
        P("rows", "rep", None, None),
        P("rows", "rep", None, None),
        P("rows", "rep", None),
        P("rows", "rep", None, None),
    )
    out_specs = (P(("rows", "rep"), None), P(("rows", "rep"), None), P(), P())
    return jax.shard_map(local, mesh=mesh, in_specs=in_specs, out_specs=out_specs, check_vma=False)
```

```python
import functools

import jax
import jax.numpy as jnp
from jax import lax
from jax.experimental import pallas as pl
from jax.experimental.pallas import tpu as pltpu
from jax.sharding import PartitionSpec as P

MESH = pl.DeviceIdType.MESH
BF = jnp.bfloat16
F32 = jnp.float32
TILE = 128
WIDTH = 256
SECTIONS = 32
SLOTS = 4
QUARTER = 512
ROWS = 2048
VMEM_LIMIT = 60 << 20


class Place:
    def __init__(self):
        rows, rep = lax.axis_index("rows"), lax.axis_index("rep")
        self.yh, x, z = rows // 16, (rows // 4) % 4, rows % 4
        self.yl, self.core = rep // 2, rep % 2
        self.a = x + self.core * (z - x)
        self.b = z + self.core * (x - z)

    def section(self, yh, a, b):
        x = a + self.core * (b - a)
        z = b + self.core * (a - b)
        return yh * 16 + x * 4 + z

    def a_peer(self, j):
        return (self.section(self.yh, (self.a + j) % 4, self.b), self.yl * 2 + self.core)

    def b_peer(self, j):
        return (self.section(self.yh, self.a, (self.b + j) % 4), self.yl * 2 + self.core)

    def y_peer(self):
        return (self.section(1 - self.yh, self.a, self.b), self.yl * 2 + self.core)

    def near_peer(self, mask):
        yh = (self.yh + mask // 4) % 2
        yl = (self.yl + (mask // 2) % 2) % 2
        core = (self.core + mask % 2) % 2
        rows, _ = lax.axis_index("rows"), None
        return (yh * 16 + rows % 16, yl * 2 + core)

    def near_id(self):
        return self.yh * 4 + self.yl * 2 + self.core

    def chunk(self, b, a):
        return b * 4 + a + self.core * (a * 4 + b - b * 4 - a)


def greet(peers):
    barrier = pltpu.get_barrier_semaphore()
    for peer in peers:
        pl.semaphore_signal(barrier, inc=1, device_id=peer, device_id_type=MESH)
    pl.semaphore_wait(barrier, len(peers))


def remote(src, dst, send, recv, peer):
    return pltpu.make_async_remote_copy(
        src_ref=src, dst_ref=dst, send_sem=send, recv_sem=recv, device_id=peer, device_id_type=MESH
    )


def masked(values, section, picks, counts):
    halves = []
    for p in range(2):
        parts = []
        for t in range(SLOTS):
            keep = jnp.logical_and(picks[section, t] == p, t < counts[0, section])
            scale = jnp.where(keep, jnp.float32(1), jnp.float32(0))
            parts.append(values[section, t] * jnp.full((TILE, TILE), scale, F32).astype(BF))
        halves.append(jnp.concatenate(parts, axis=0))
    return jnp.concatenate(halves, axis=1)


def layer_kernel(
    features, values_hbm, weight, bias, cotangent, pull_vec, rows, picks, counts, pulls,
    act, fgrad, wgrad, bgrad, *scratch,
):
    dense, scratch = scratch[:8], scratch[8:]
    (values, asked, wants, packed, got, running, last,
     swap_out, from_core, to_near, from_near, back,
     terms, from_b, to_y, from_y, to_a, from_a, held,
     w0, w1, s1, w2, s2, w3, s4, w5,
     load_sem, own_sem, want_sem, ask_send, ask_recv,
     fa_send, fa_recv, fy_send, fy_recv, fb_send, fb_recv,
     core_send, core_recv, near_send, near_recv,
     gc_send, gc_recv, gn_send, gn_recv, gf_send, gf_recv,
     b_send, b_recv, y_send, y_recv, a_send, a_recv,
     w1_send, w1_recv, w2_send, w2_recv, w3_send, w3_recv, w4_send, w4_recv, w5_send, w5_recv) = scratch
    me = Place()
    fetch = pltpu.make_async_copy(
        features.at[pl.ds((me.yl * 2 + me.core) * 4, 4)], dense[0], own_sem
    )
    fetch.start()
    load = pltpu.make_async_copy(values_hbm, values, load_sem)
    load.start()
    greet(
        [me.near_peer(m) for m in range(1, 8)]
        + [me.a_peer(j) for j in (1, 2, 3)]
        + [me.b_peer(j) for j in (1, 2, 3)]
    )

    def ask(j):
        return remote(pull_vec, asked.at[j - 1], ask_send.at[j - 1], ask_recv.at[j - 1], me.b_peer(j))

    for j in (1, 2, 3):
        ask(j).start()
    fetch.wait()

    def along(j):
        return remote(dense[0], dense[j], fa_send.at[j - 1], fa_recv.at[j - 1], me.a_peer(j))

    def across(j):
        return remote(dense[j], dense[4 + j], fy_send.at[j], fy_recv.at[j], me.y_peer())

    def give(n, to):
        return remote(
            packed.at[to - 1, n], got.at[to, n], fb_send.at[to - 1, n], fb_recv.at[to - 1, n], me.b_peer(to)
        )

    def block_section(n, b):
        return me.section((me.yh + n // 4) % 2, (me.a + 4 - n % 4) % 4, b)

    for j in (1, 3, 2):
        along(j).start()
    across(0).start()
    for j in (1, 2, 3):
        ask(j).wait()
        table = pltpu.make_async_copy(asked.at[j - 1], wants.at[j - 1], want_sem)
        table.start()
        table.wait()

    def serve(n):
        column = block_section(n, me.b)
        for source in (1, 3, 2):
            to = 4 - source
            for p in range(2):
                packed[to - 1, n, p] = dense[n][wants[source - 1, column, p]]
            give(n, to).start()
        for p in range(2):
            got[0, n, p] = dense[n][pulls[column, p]]

    serve(0)
    for j in (1, 3, 2):
        along(j).wait_recv()
        across(j).start()
        serve(j)
    for j in (0, 1, 3, 2):
        across(j).wait_recv()
        serve(4 + j)

    load.wait()
    running[128] = jnp.zeros((TILE, WIDTH), F32)

    def forward(step, carry):
        ends = list(carry)
        n = step // 4 * 4 + (step % 4 + (step % 4) // 2 * (5 - 2 * (step % 4)))
        for j in (1, 2, 3):
            give(n, j).wait_recv()
        for source in range(4):
            section = block_section(n, (me.b + 4 - source) % 4)
            block = got[source, n].reshape(2 * TILE, WIDTH)
            sums = jnp.dot(masked(values, section, picks, counts), block, preferred_element_type=F32)
            for t in range(SLOTS):
                row = rows[section, t]
                before = jnp.int32(128)
                slot = (step * 4 + source) * 4 + t
                for r in range(16):
                    before = jnp.where(row == r, ends[r], before)
                    ends[r] = jnp.where(row == r, slot, ends[r])
                running[slot] = sums[t * TILE:(t + 1) * TILE] + running[before]
        return tuple(ends)

    ends = lax.fori_loop(0, 8, forward, (jnp.int32(128),) * 16)
    for r in range(16):
        last[r] = ends[r]

    def part(r):
        return running[last[r]]

    core_peer, near_peer = me.near_peer(1), me.near_peer(2)
    quarters = [(1 - me.yl) * 2, me.yl * 2]

    def swap(n, t):
        return remote(swap_out.at[n, t], from_core.at[n, t], core_send.at[n, t], core_recv.at[n, t], core_peer)

    def over(t):
        return remote(to_near.at[t], from_near.at[t], near_send.at[t], near_recv.at[t], near_peer)

    for n in range(2):
        for t in range(4):
            swap_out[n, t] = part((quarters[n] + 1 - me.core) * 4 + t)
            swap(n, t).start()
    for t in range(4):
        swap(0, t).wait_recv()
        to_near[t] = (part((quarters[0] + me.core) * 4 + t) + from_core[0, t]).astype(BF)
        over(t).start()

    mine = me.yl * 2 + me.core
    yours = (1 - me.yl) * 2 + me.core

    def share_core(t):
        ref = back.at[mine * 4 + t]
        return remote(ref, ref, gc_send.at[t], gc_recv.at[t], core_peer)

    def share_near(t):
        ref = back.at[mine * 4 + t]
        return remote(ref, ref, gn_send.at[t], gn_recv.at[t], near_peer)

    def forward_on(t):
        ref = back.at[yours * 4 + t]
        return remote(ref, ref, gf_send.at[t], gf_recv.at[t], core_peer)

    grad = jnp.zeros((WIDTH, WIDTH), F32)
    bias_sum = jnp.zeros((1, WIDTH), F32)
    for t in range(4):
        swap(1, t).wait_recv()
        over(t).wait_recv()
        agg = (part(mine * 4 + t) + from_core[1, t] + from_near[t].astype(F32)).astype(BF)
        pre = jnp.dot(agg, weight[...], preferred_element_type=F32) + bias[...]
        sig = 1.0 / (1.0 + jnp.exp(-pre))
        act[t] = (pre * sig).astype(BF)
        slope = (cotangent[t].astype(F32) * (sig * (1.0 + pre * (1.0 - sig)))).astype(BF)
        back[mine * 4 + t] = lax.dot_general(
            slope, weight[...], (((1,), (1,)), ((), ())), preferred_element_type=F32
        ).astype(BF)
        share_near(t).start()
        share_core(t).start()
        grad += lax.dot_general(agg, slope, (((0,), (0,)), ((), ())), preferred_element_type=F32)
        bias_sum += jnp.sum(slope.astype(F32), axis=0, keepdims=True)

    for c in range(16):
        b, a = c // 4, c % 4
        w0[b + me.core * (a - b), a + me.core * (b - a), :16] = grad[c * 16:(c + 1) * 16]
        w0[b, a, 16:24] = jnp.zeros((8, WIDTH), F32)
    w0[0, 0, 16:17] = bias_sum

    def w1_copy(j):
        return remote(w0.at[(me.b + j) % 4], w1.at[j - 1], w1_send.at[j - 1], w1_recv.at[j - 1], me.b_peer(j))

    def w2_copy(j):
        return remote(s1.at[(me.a + j) % 4], w2.at[j - 1], w2_send.at[j - 1], w2_recv.at[j - 1], me.a_peer(j))

    def w3_copy(m):
        return remote(s2, w3.at[me.near_id()], w3_send.at[m - 1], w3_recv.at[m - 1], me.near_peer(m))

    def w4_copy(j):
        return remote(s4.at[me.a], s4.at[me.a], w4_send.at[j - 1], w4_recv.at[j - 1], me.a_peer(j))

    def w5_copy(j):
        return remote(s4, w5.at[me.b], w5_send.at[j - 1], w5_recv.at[j - 1], me.b_peer(j))

    for j in (1, 2, 3):
        w1_copy(j).start()

    for t in range(4):
        share_near(t).wait_recv()
        forward_on(t).start()
    for t in range(4):
        share_core(t).wait()
        forward_on(t).wait()

    def place(k):
        return (me.yh + 1 + k // 4) % 2, (me.a + 1 + k % 4) % 4

    def send_b(k, j):
        return remote(
            terms.at[j, k], from_b.at[j - 1, k], b_send.at[j - 1, k], b_recv.at[j - 1, k], me.b_peer(j)
        )

    def products(k, j):
        yh, a = place(k)
        section = me.section(yh, a, (me.b + j) % 4)
        sources = jnp.concatenate([back[rows[section, t]] for t in range(SLOTS)], axis=0)
        terms[j, k] = lax.dot_general(
            masked(values, section, picks, counts), sources, (((0,), (0,)), ((), ())),
            preferred_element_type=F32,
        ).astype(BF)

    def contribute(k, carry):
        for j in (1, 3, 2):
            products(k, j)
            send_b(k, j).start()
        return carry

    def keep(k, carry):
        products(k, 0)
        return carry

    lax.fori_loop(0, 8, contribute, 0)
    lax.fori_loop(0, 8, keep, 0)

    def send_y(k):
        return remote(to_y.at[k], from_y.at[k], y_send.at[k], y_recv.at[k], me.y_peer())

    def send_a(k):
        return remote(to_a.at[k], from_a.at[k], a_send.at[k], a_recv.at[k], me.a_peer(1 + k))

    def gather_b(k, q):
        yh, a = place(k)
        section = me.section(yh, a, me.b)
        sums = jnp.zeros((TILE, WIDTH), F32)
        for source in range(4):
            for p in range(2):
                if source == 0:
                    hit, tile = pulls[section, p] == q, terms[0, k, p * TILE:(p + 1) * TILE]
                else:
                    hit = wants[source - 1, section, p] == q
                    tile = from_b[source - 1, k, p * TILE:(p + 1) * TILE]
                sums += tile.astype(F32) * jnp.where(hit, jnp.float32(1), jnp.float32(0))
        return sums

    def arrive_b(k):
        for j in (1, 2, 3):
            send_b(k, j).wait_recv()

    def other_half(k):
        arrive_b(k)

        def column(q, inner):
            to_y[k, q] = gather_b(k, q).astype(BF)
            return inner

        lax.fori_loop(0, 4, column, 0)
        send_y(k).start()

    def this_half(k):
        arrive_b(4 + k)
        send_y(k).wait_recv()

        def column(q, inner):
            sums = gather_b(4 + k, q) + from_y[k, q].astype(F32)
            if k < 3:
                to_a[k, q] = sums.astype(BF)
            else:
                held[q] = sums
            return inner

        lax.fori_loop(0, 4, column, 0)
        if k < 3:
            send_a(k).start()

    other_half(0)
    for j in (1, 2, 3):
        w1_copy(j).wait()
    s1[...] = w0[me.b] + w1[0] + w1[1] + w1[2]
    for j in (1, 2, 3):
        w2_copy(j).start()
    other_half(1)
    other_half(2)
    for j in (1, 2, 3):
        w2_copy(j).wait()
    s2[...] = s1[me.a] + w2[0] + w2[1] + w2[2]
    for m in range(1, 8):
        w3_copy(m).start()
    w3[me.near_id()] = s2[...]
    other_half(3)
    this_half(0)
    for m in range(1, 8):
        w3_copy(m).wait()
    total = w3[0]
    for m in range(1, 8):
        total = total + w3[m]
    s4[me.a] = total
    for j in (1, 2, 3):
        w4_copy(j).start()
    this_half(1)
    this_half(2)
    for j in (1, 2, 3):
        w4_copy(j).wait()
    for j in (1, 2, 3):
        w5_copy(j).start()
    w5[me.b] = s4[...]
    this_half(3)
    for j in (1, 2, 3):
        w5_copy(j).wait()
    for b in range(4):
        for a in range(4):
            wgrad[me.chunk(b, a)] = w5[b, a, :16]
    bgrad[...] = w5[0, 0, 16:17]
    for k in range(3):
        send_a(k).wait_recv()
    for q in range(4):
        fgrad[q] = held[q] + from_a[0, q].astype(F32) + from_a[1, q].astype(F32) + from_a[2, q].astype(F32)

    for j in (1, 2, 3):
        along(j).wait_send()
    for j in range(4):
        across(j).wait_send()
        over(j).wait_send()
        share_near(j).wait_send()
        send_y(j).wait_send()
        for n in range(2):
            swap(n, j).wait_send()
    for k in range(3):
        send_a(k).wait_send()

    def drain(n, carry):
        for j in (1, 2, 3):
            give(n, j).wait_send()
            send_b(n, j).wait_send()
        return carry

    lax.fori_loop(0, 8, drain, 0)


def layer(features, values, weight, bias, cotangent, rows, picks, counts, pulls):
    dma = pltpu.SemaphoreType.DMA
    vmem, smem = pl.BlockSpec(memory_space=pltpu.VMEM), pl.BlockSpec(memory_space=pltpu.SMEM)
    hbm = pl.BlockSpec(memory_space=pl.ANY)
    return pl.pallas_call(
        layer_kernel,
        name="layer",
        out_shape=(
            jax.ShapeDtypeStruct((4, TILE, WIDTH), BF),
            jax.ShapeDtypeStruct((4, TILE, WIDTH), F32),
            jax.ShapeDtypeStruct((16, 16, WIDTH), F32),
            jax.ShapeDtypeStruct((1, WIDTH), F32),
        ),
        in_specs=[hbm, hbm, vmem, vmem, vmem, vmem, smem, smem, smem, smem],
        out_specs=(vmem,) * 4,
        scratch_shapes=[
            *[pltpu.VMEM((4, TILE, WIDTH), BF)] * 8,
            pltpu.VMEM((SECTIONS, SLOTS, TILE, TILE), BF),
            pltpu.VMEM((3, SECTIONS, 2), jnp.int32),
            pltpu.SMEM((3, SECTIONS, 2), jnp.int32),
            pltpu.VMEM((3, 8, 2, TILE, WIDTH), BF),
            pltpu.VMEM((4, 8, 2, TILE, WIDTH), BF),
            pltpu.VMEM((129, TILE, WIDTH), F32),
            pltpu.SMEM((16,), jnp.int32),
            pltpu.VMEM((2, 4, TILE, WIDTH), F32),
            pltpu.VMEM((2, 4, TILE, WIDTH), F32),
            pltpu.VMEM((4, TILE, WIDTH), BF),
            pltpu.VMEM((4, TILE, WIDTH), BF),
            pltpu.VMEM((16, TILE, WIDTH), BF),
            pltpu.VMEM((4, 8, 2 * TILE, WIDTH), BF),
            pltpu.VMEM((3, 8, 2 * TILE, WIDTH), BF),
            pltpu.VMEM((4, 4, TILE, WIDTH), BF),
            pltpu.VMEM((4, 4, TILE, WIDTH), BF),
            pltpu.VMEM((3, 4, TILE, WIDTH), BF),
            pltpu.VMEM((3, 4, TILE, WIDTH), BF),
            pltpu.VMEM((4, TILE, WIDTH), F32),
            pltpu.VMEM((4, 4, 24, WIDTH), F32),
            pltpu.VMEM((3, 4, 24, WIDTH), F32),
            pltpu.VMEM((4, 24, WIDTH), F32),
            pltpu.VMEM((3, 24, WIDTH), F32),
            pltpu.VMEM((24, WIDTH), F32),
            pltpu.VMEM((8, 24, WIDTH), F32),
            pltpu.VMEM((4, 24, WIDTH), F32),
            pltpu.VMEM((4, 4, 24, WIDTH), F32),
            dma, dma, dma, dma((3,)), dma((3,)),
            dma((3,)), dma((3,)), dma((4,)), dma((4,)), dma((3, 8)), dma((3, 8)),
            dma((2, 4)), dma((2, 4)), dma((4,)), dma((4,)),
            dma((4,)), dma((4,)), dma((4,)), dma((4,)), dma((4,)), dma((4,)),
            dma((3, 8)), dma((3, 8)), dma((4,)), dma((4,)), dma((3,)), dma((3,)),
            dma((3,)), dma((3,)), dma((3,)), dma((3,)), dma((7,)), dma((7,)),
            dma((3,)), dma((3,)), dma((3,)), dma((3,)),
        ],
        compiler_params=pltpu.CompilerParams(
            collective_id=1, has_side_effects=True, vmem_limit_bytes=VMEM_LIMIT
        ),
    )(
        features.reshape(16, TILE, WIDTH), values, weight, bias.reshape(1, WIDTH),
        cotangent.reshape(4, TILE, WIDTH), pulls, rows, picks, counts, pulls,
    )


def local(
    features, weight, bias, cotangent, tile_vals, tile_rows, tile_pick, tile_count, pull_cols
):
    act, fgrad, wgrad, bgrad = layer(
        features,
        tile_vals.reshape(SECTIONS, SLOTS, TILE, TILE),
        weight,
        bias,
        cotangent,
        tile_rows.reshape(SECTIONS, SLOTS),
        tile_pick.reshape(SECTIONS, SLOTS),
        tile_count.reshape(1, SECTIONS),
        pull_cols.reshape(SECTIONS, 2),
    )
    return (
        act.reshape(QUARTER, WIDTH),
        fgrad.reshape(QUARTER, WIDTH),
        wgrad.reshape(WIDTH, WIDTH),
        bgrad.reshape(WIDTH),
    )


def solution(mesh):
    in_specs = (
        P("rows", None),
        P(),
        P(),
        P(("rows", "rep"), None),
        P("rows", "rep", None, None, None, None),
        P("rows", "rep", None, None),
        P("rows", "rep", None, None),
        P("rows", "rep", None),
        P("rows", "rep", None, None),
    )
    out_specs = (P(("rows", "rep"), None), P(("rows", "rep"), None), P(), P())
    return jax.shard_map(local, mesh=mesh, in_specs=in_specs, out_specs=out_specs, check_vma=False)
```

```python
import functools

import jax
import jax.numpy as jnp
from jax import lax
from jax.experimental import pallas as pl
from jax.experimental.pallas import tpu as pltpu
from jax.sharding import PartitionSpec as P

MESH = pl.DeviceIdType.MESH
BF = jnp.bfloat16
F32 = jnp.float32
TILE = 128
WIDTH = 256
SECTIONS = 32
SLOTS = 4
QUARTER = 512
ROWS = 2048
VMEM_LIMIT = 60 << 20


class Place:
    def __init__(self):
        rows, rep = lax.axis_index("rows"), lax.axis_index("rep")
        self.yh, x, z = rows // 16, (rows // 4) % 4, rows % 4
        self.x, self.z = x, z
        self.yl, self.core = rep // 2, rep % 2
        self.a = x + self.core * (z - x)
        self.b = z + self.core * (x - z)

    def section(self, yh, a, b):
        x = a + self.core * (b - a)
        z = b + self.core * (a - b)
        return yh * 16 + x * 4 + z

    def a_peer(self, j):
        return (self.section(self.yh, (self.a + j) % 4, self.b), self.yl * 2 + self.core)

    def b_peer(self, j):
        return (self.section(self.yh, self.a, (self.b + j) % 4), self.yl * 2 + self.core)

    def y_peer(self):
        return (self.section(1 - self.yh, self.a, self.b), self.yl * 2 + self.core)

    def near_peer(self, mask):
        yh = (self.yh + mask // 4) % 2
        yl = (self.yl + (mask // 2) % 2) % 2
        core = (self.core + mask % 2) % 2
        rows = lax.axis_index("rows")
        return (yh * 16 + rows % 16, yl * 2 + core)

    def near_id(self):
        return self.yh * 4 + self.yl * 2 + self.core

    def x_peer(self, j):
        rows = lax.axis_index("rows")
        return (self.yh * 16 + (rows + 4 * j) % 16, self.yl * 2 + self.core)

    def z_peer(self, j):
        rows = lax.axis_index("rows")
        return (rows // 4 * 4 + (rows + j) % 4, self.yl * 2 + self.core)


def greet(peers):
    barrier = pltpu.get_barrier_semaphore()
    for peer in peers:
        pl.semaphore_signal(barrier, inc=1, device_id=peer, device_id_type=MESH)
    pl.semaphore_wait(barrier, len(peers))


def remote(src, dst, send, recv, peer):
    return pltpu.make_async_remote_copy(
        src_ref=src, dst_ref=dst, send_sem=send, recv_sem=recv, device_id=peer, device_id_type=MESH
    )


def masked(values, section, picks, counts):
    halves = []
    for p in range(2):
        parts = []
        for t in range(SLOTS):
            keep = jnp.logical_and(picks[t, section] == p, t < counts[0, section])
            scale = jnp.where(keep, jnp.float32(1), jnp.float32(0))
            parts.append(values[section, t] * jnp.full((TILE, TILE), scale, F32).astype(BF))
        halves.append(jnp.concatenate(parts, axis=0))
    return jnp.concatenate(halves, axis=1)


def layer_kernel(
    features, values_hbm, weight_hbm, bias, cot_hbm, pull_vec, rows, picks, counts, pulls,
    act_out, fgrad_out, wgrad_out, bgrad, *scratch,
):
    dense, scratch = scratch[:8], scratch[8:]
    (values, weight, cotangent, asked, wants, packed, got, running, last,
     swap_out, from_core, to_near, from_near, agg_all, slope_all, act, back,
     terms, from_b, to_y, from_y, to_a, from_a, held, fgrad,
     w0, n1, s1, w2, s2, w3, s4, wgrad, b1, x1, b2, z1,
     load_sem, weight_sem, cot_sem, own_sem, want_sem, act_sem, fgrad_sem, wgrad_sem, ask_send, ask_recv,
     fa_send, fa_recv, fy_send, fy_recv, fb_send, fb_recv,
     core_send, core_recv, near_send, near_recv,
     gc_send, gc_recv, gn_send, gn_recv, gf_send, gf_recv,
     b_send, b_recv, y_send, y_recv, a_send, a_recv,
     n1_send, n1_recv, w2_send, w2_recv, w3_send, w3_recv, w4_send, w4_recv, w5_send, w5_recv,
     x1_send, x1_recv, z1_send, z1_recv) = scratch
    me = Place()
    fetch = pltpu.make_async_copy(
        features.at[pl.ds((me.yl * 2 + me.core) * 4, 4)], dense[0], own_sem
    )
    fetch.start()
    loads = [
        pltpu.make_async_copy(values_hbm, values, load_sem),
        pltpu.make_async_copy(weight_hbm, weight, weight_sem),
        pltpu.make_async_copy(cot_hbm, cotangent, cot_sem),
    ]
    for load in loads:
        load.start()
    greet(
        [me.near_peer(m) for m in range(1, 8)]
        + [me.a_peer(j) for j in (1, 2, 3)]
        + [me.b_peer(j) for j in (1, 2, 3)]
    )

    def ask(j):
        return remote(pull_vec, asked.at[j - 1], ask_send.at[j - 1], ask_recv.at[j - 1], me.b_peer(j))

    for j in (1, 2, 3):
        ask(j).start()
    fetch.wait()

    def along(j):
        return remote(dense[0], dense[j], fa_send.at[j - 1], fa_recv.at[j - 1], me.a_peer(j))

    def across(j):
        return remote(dense[j], dense[4 + j], fy_send.at[j], fy_recv.at[j], me.y_peer())

    def give(n, to):
        return remote(
            packed.at[to - 1, n], got.at[to, n], fb_send.at[to - 1, n], fb_recv.at[to - 1, n], me.b_peer(to)
        )

    def block_section(n, b):
        return me.section((me.yh + n // 4) % 2, (me.a + 4 - n % 4) % 4, b)

    for j in (1, 3, 2):
        along(j).start()
    across(0).start()
    for j in (1, 2, 3):
        ask(j).wait()
        table = pltpu.make_async_copy(asked.at[j - 1], wants.at[j - 1], want_sem)
        table.start()
        table.wait()

    def serve(n):
        column = block_section(n, me.b)
        for source in (1, 3, 2):
            to = 4 - source
            for p in range(2):
                packed[to - 1, n, p] = dense[n][wants[source - 1, p, column]]
            give(n, to).start()
        for p in range(2):
            got[0, n, p] = dense[n][pulls[p, column]]

    serve(0)
    for j in (1, 3, 2):
        along(j).wait_recv()
        across(j).start()
        serve(j)
    for j in (0, 1, 3, 2):
        across(j).wait_recv()
        serve(4 + j)

    for load in loads:
        load.wait()
    running[128] = jnp.zeros((TILE, WIDTH), F32)

    def forward(step, carry):
        ends = list(carry)
        n = step // 4 * 4 + (step % 4 + (step % 4) // 2 * (5 - 2 * (step % 4)))
        for j in (1, 2, 3):
            give(n, j).wait_recv()
        for source in range(4):
            section = block_section(n, (me.b + 4 - source) % 4)
            block = got[source, n].reshape(2 * TILE, WIDTH)
            sums = jnp.dot(masked(values, section, picks, counts), block, preferred_element_type=F32)
            for t in range(SLOTS):
                row = rows[t, section]
                before = jnp.int32(128)
                slot = (step * 4 + source) * 4 + t
                for r in range(16):
                    before = jnp.where(row == r, ends[r], before)
                    ends[r] = jnp.where(row == r, slot, ends[r])
                running[slot] = sums[t * TILE:(t + 1) * TILE] + running[before]
        return tuple(ends)

    ends = lax.fori_loop(0, 8, forward, (jnp.int32(128),) * 16)
    for r in range(16):
        last[r] = ends[r]

    def part(r):
        return running[last[r]]

    core_peer, near_peer = me.near_peer(1), me.near_peer(2)
    quarters = [(1 - me.yl) * 2, me.yl * 2]

    def swap(n, t):
        return remote(swap_out.at[n, t], from_core.at[n, t], core_send.at[n, t], core_recv.at[n, t], core_peer)

    def over(t):
        return remote(to_near.at[t], from_near.at[t], near_send.at[t], near_recv.at[t], near_peer)

    for n in range(2):
        for t in range(4):
            swap_out[n, t] = part((quarters[n] + 1 - me.core) * 4 + t)
            swap(n, t).start()
    for t in range(4):
        swap(0, t).wait_recv()
        to_near[t] = (part((quarters[0] + me.core) * 4 + t) + from_core[0, t]).astype(BF)
        over(t).start()

    mine = me.yl * 2 + me.core
    yours = (1 - me.yl) * 2 + me.core

    def share_core(t):
        ref = back.at[mine * 4 + t]
        return remote(ref, ref, gc_send.at[t], gc_recv.at[t], core_peer)

    def share_near(t):
        ref = back.at[mine * 4 + t]
        return remote(ref, ref, gn_send.at[t], gn_recv.at[t], near_peer)

    def forward_on(t):
        ref = back.at[yours * 4 + t]
        return remote(ref, ref, gf_send.at[t], gf_recv.at[t], core_peer)

    for t in range(4):
        swap(1, t).wait_recv()
        over(t).wait_recv()
        agg = (part(mine * 4 + t) + from_core[1, t] + from_near[t].astype(F32)).astype(BF)
        agg_all[t * TILE:(t + 1) * TILE] = agg
        pre = jnp.dot(agg, weight[...], preferred_element_type=F32) + bias[...]
        sig = 1.0 / (1.0 + jnp.exp(-pre))
        act[t] = (pre * sig).astype(BF)
        slope = (cotangent[t].astype(F32) * (sig * (1.0 + pre * (1.0 - sig)))).astype(BF)
        slope_all[t * TILE:(t + 1) * TILE] = slope
        back[mine * 4 + t] = lax.dot_general(
            slope, weight[...], (((1,), (1,)), ((), ())), preferred_element_type=F32
        ).astype(BF)
        share_near(t).start()
        share_core(t).start()
    give_act = pltpu.make_async_copy(act, act_out, act_sem)
    give_act.start()

    grad = lax.dot_general(
        agg_all[...], slope_all[...], (((0,), (0,)), ((), ())), preferred_element_type=F32
    )
    bias_sum = jnp.sum(slope_all[...].astype(F32), axis=0, keepdims=True)
    for m in range(8):
        w0[m, :32] = grad[m * 32:(m + 1) * 32]
        w0[m, 32:40] = jnp.broadcast_to(bias_sum, (8, WIDTH))

    def n1_copy(m):
        other = (me.yh + m // 4) % 2 * 4 + (me.yl + m // 2 % 2) % 2 * 2 + (me.core + m % 2) % 2
        return remote(
            w0.at[other], n1.at[me.near_id()], n1_send.at[m - 1], n1_recv.at[m - 1], me.near_peer(m)
        )

    def w2_copy(j):
        return remote(
            s1.at[(me.a + j) % 4], w2.at[me.a], w2_send.at[j - 1], w2_recv.at[j - 1], me.a_peer(j)
        )

    def x1_copy(j):
        return remote(b1, x1.at[me.x], x1_send.at[j - 1], x1_recv.at[j - 1], me.x_peer(j))

    def w3_copy(j):
        return remote(s2, w3.at[me.b], w3_send.at[j - 1], w3_recv.at[j - 1], me.b_peer(j))

    def z1_copy(j):
        return remote(b2, z1.at[me.z], z1_send.at[j - 1], z1_recv.at[j - 1], me.z_peer(j))

    def w4_copy(j):
        return remote(s4.at[me.a], s4.at[me.a], w4_send.at[j - 1], w4_recv.at[j - 1], me.a_peer(j))

    def w5_copy(m):
        ref = wgrad.at[me.near_id()]
        return remote(ref, ref, w5_send.at[m - 1], w5_recv.at[m - 1], me.near_peer(m))

    for m in range(1, 8):
        n1_copy(m).start()
    n1[me.near_id()] = w0[me.near_id()]

    def weight_over_a():
        for m in range(1, 8):
            n1_copy(m).wait()
        total = n1[0]
        for m in range(1, 8):
            total = total + n1[m]
        for a in range(4):
            s1[a] = total[a * 8:(a + 1) * 8]
        b1[...] = total[32:40]
        for j in (1, 2, 3):
            w2_copy(j).start()
            x1_copy(j).start()
        w2[me.a] = s1[me.a]
        x1[me.x] = b1[...]

    def weight_over_b():
        for j in (1, 2, 3):
            w2_copy(j).wait()
            x1_copy(j).wait()
        s2[...] = w2[0] + w2[1] + w2[2] + w2[3]
        b2[...] = x1[0] + x1[1] + x1[2] + x1[3]
        for j in (1, 2, 3):
            w3_copy(j).start()
            z1_copy(j).start()
        w3[me.b] = s2[...]
        z1[me.z] = b2[...]

    def weight_back_a():
        for j in (1, 2, 3):
            w3_copy(j).wait()
            z1_copy(j).wait()
        s4[me.a] = w3[0] + w3[1] + w3[2] + w3[3]
        bgrad[...] = (z1[0] + z1[1] + z1[2] + z1[3])[:1]
        for j in (1, 2, 3):
            w4_copy(j).start()

    def weight_back_near():
        for j in (1, 2, 3):
            w4_copy(j).wait()
        wgrad[me.near_id()] = s4[...].reshape(32, WIDTH)
        for m in range(1, 8):
            w5_copy(m).start()

    for t in range(4):
        share_near(t).wait_recv()
        forward_on(t).start()
    for t in range(4):
        share_core(t).wait()
        forward_on(t).wait()

    def place(k):
        return (me.yh + 1 + k // 4) % 2, (me.a + 1 + k % 4) % 4

    def send_b(k, j):
        return remote(
            terms.at[j, k], from_b.at[j - 1, k], b_send.at[j - 1, k], b_recv.at[j - 1, k], me.b_peer(j)
        )

    def products(k, j):
        yh, a = place(k)
        section = me.section(yh, a, (me.b + j) % 4)
        sources = jnp.concatenate([back[rows[t, section]] for t in range(SLOTS)], axis=0)
        terms[j, k] = lax.dot_general(
            masked(values, section, picks, counts), sources, (((0,), (0,)), ((), ())),
            preferred_element_type=F32,
        ).astype(BF)

    def contribute(k):
        for j in (1, 3, 2):
            products(k, j)
            send_b(k, j).start()

    def send_y(k):
        return remote(to_y.at[k], from_y.at[k], y_send.at[k], y_recv.at[k], me.y_peer())

    def send_a(k):
        return remote(to_a.at[k], from_a.at[k], a_send.at[k], a_recv.at[k], me.a_peer(1 + k))

    def gather_b(k, q):
        yh, a = place(k)
        section = me.section(yh, a, me.b)
        sums = jnp.zeros((TILE, WIDTH), F32)
        for source in range(4):
            for p in range(2):
                if source == 0:
                    hit, tile = pulls[p, section] == q, terms[0, k, p * TILE:(p + 1) * TILE]
                else:
                    hit = wants[source - 1, p, section] == q
                    tile = from_b[source - 1, k, p * TILE:(p + 1) * TILE]
                sums += tile.astype(F32) * jnp.where(hit, jnp.float32(1), jnp.float32(0))
        return sums

    def arrive_b(k):
        for j in (1, 2, 3):
            send_b(k, j).wait_recv()

    def start(k, carry):
        contribute(k)
        return carry

    def other_half(k, carry):
        products(k, 0)
        arrive_b(k)

        def column(q, inner):
            to_y[k, q] = gather_b(k, q).astype(BF)
            return inner

        lax.fori_loop(0, 4, column, 0)
        send_y(k).start()
        contribute(4 + k)
        pl.when(k == 0)(weight_over_a)
        pl.when(k == 2)(weight_over_b)
        return carry

    def this_half(k, carry):
        products(4 + k, 0)
        arrive_b(4 + k)
        send_y(k).wait_recv()

        def column(q, inner):
            sums = gather_b(4 + k, q) + from_y[k, q].astype(F32)
            to_a[k, q] = sums.astype(BF)
            held[q] = sums
            return inner

        lax.fori_loop(0, 4, column, 0)

        @pl.when(k < 3)
        def _():
            send_a(k).start()

        pl.when(k == 0)(weight_back_a)
        pl.when(k == 2)(weight_back_near)
        return carry

    lax.fori_loop(0, 4, start, 0)
    lax.fori_loop(0, 4, other_half, 0)
    lax.fori_loop(0, 4, this_half, 0)
    for m in range(1, 8):
        w5_copy(m).wait()
    give_wgrad = pltpu.make_async_copy(wgrad, wgrad_out, wgrad_sem)
    give_wgrad.start()
    for k in range(3):
        send_a(k).wait_recv()
    for q in range(4):
        fgrad[q] = held[q] + from_a[0, q].astype(F32) + from_a[1, q].astype(F32) + from_a[2, q].astype(F32)
    give_fgrad = pltpu.make_async_copy(fgrad, fgrad_out, fgrad_sem)
    give_fgrad.start()

    for j in (1, 2, 3):
        along(j).wait_send()
    for j in range(4):
        across(j).wait_send()
        over(j).wait_send()
        share_near(j).wait_send()
        send_y(j).wait_send()
        for n in range(2):
            swap(n, j).wait_send()
    for k in range(3):
        send_a(k).wait_send()

    def drain(n, carry):
        for j in (1, 2, 3):
            give(n, j).wait_send()
            send_b(n, j).wait_send()
        return carry

    lax.fori_loop(0, 8, drain, 0)
    give_act.wait()
    give_wgrad.wait()
    give_fgrad.wait()


def layer(features, values, weight, bias, cotangent, rows, picks, counts, pulls):
    dma = pltpu.SemaphoreType.DMA
    vmem, smem = pl.BlockSpec(memory_space=pltpu.VMEM), pl.BlockSpec(memory_space=pltpu.SMEM)
    hbm = pl.BlockSpec(memory_space=pl.ANY)
    return pl.pallas_call(
        layer_kernel,
        name="layer",
        out_shape=(
            jax.ShapeDtypeStruct((4, TILE, WIDTH), BF),
            jax.ShapeDtypeStruct((4, TILE, WIDTH), F32),
            jax.ShapeDtypeStruct((8, 32, WIDTH), F32),
            jax.ShapeDtypeStruct((1, WIDTH), F32),
        ),
        in_specs=[hbm, hbm, hbm, vmem, hbm, vmem, smem, smem, smem, smem],
        out_specs=(hbm, hbm, hbm, vmem),
        scratch_shapes=[
            *[pltpu.VMEM((4, TILE, WIDTH), BF)] * 8,
            pltpu.VMEM((SECTIONS, SLOTS, TILE, TILE), BF),
            pltpu.VMEM((WIDTH, WIDTH), BF),
            pltpu.VMEM((4, TILE, WIDTH), BF),
            pltpu.VMEM((3, 2, SECTIONS), jnp.int32),
            pltpu.SMEM((3, 2, SECTIONS), jnp.int32),
            pltpu.VMEM((3, 8, 2, TILE, WIDTH), BF),
            pltpu.VMEM((4, 8, 2, TILE, WIDTH), BF),
            pltpu.VMEM((129, TILE, WIDTH), F32),
            pltpu.SMEM((16,), jnp.int32),
            pltpu.VMEM((2, 4, TILE, WIDTH), F32),
            pltpu.VMEM((2, 4, TILE, WIDTH), F32),
            pltpu.VMEM((4, TILE, WIDTH), BF),
            pltpu.VMEM((4, TILE, WIDTH), BF),
            pltpu.VMEM((QUARTER, WIDTH), BF),
            pltpu.VMEM((QUARTER, WIDTH), BF),
            pltpu.VMEM((4, TILE, WIDTH), BF),
            pltpu.VMEM((16, TILE, WIDTH), BF),
            pltpu.VMEM((4, 8, 2 * TILE, WIDTH), BF),
            pltpu.VMEM((3, 8, 2 * TILE, WIDTH), BF),
            pltpu.VMEM((4, 4, TILE, WIDTH), BF),
            pltpu.VMEM((4, 4, TILE, WIDTH), BF),
            pltpu.VMEM((4, 4, TILE, WIDTH), BF),
            pltpu.VMEM((3, 4, TILE, WIDTH), BF),
            pltpu.VMEM((4, TILE, WIDTH), F32),
            pltpu.VMEM((4, TILE, WIDTH), F32),
            pltpu.VMEM((8, 40, WIDTH), F32),
            pltpu.VMEM((8, 40, WIDTH), F32),
            pltpu.VMEM((4, 8, WIDTH), F32),
            pltpu.VMEM((4, 8, WIDTH), F32),
            pltpu.VMEM((8, WIDTH), F32),
            pltpu.VMEM((4, 8, WIDTH), F32),
            pltpu.VMEM((4, 8, WIDTH), F32),
            pltpu.VMEM((8, 32, WIDTH), F32),
            pltpu.VMEM((8, WIDTH), F32),
            pltpu.VMEM((4, 8, WIDTH), F32),
            pltpu.VMEM((8, WIDTH), F32),
            pltpu.VMEM((4, 8, WIDTH), F32),
            *[dma] * 8, dma((3,)), dma((3,)),
            dma((3,)), dma((3,)), dma((4,)), dma((4,)), dma((3, 8)), dma((3, 8)),
            dma((2, 4)), dma((2, 4)), dma((4,)), dma((4,)),
            dma((4,)), dma((4,)), dma((4,)), dma((4,)), dma((4,)), dma((4,)),
            dma((3, 8)), dma((3, 8)), dma((4,)), dma((4,)), dma((3,)), dma((3,)),
            dma((7,)), dma((7,)), dma((3,)), dma((3,)), dma((3,)), dma((3,)),
            dma((3,)), dma((3,)), dma((7,)), dma((7,)),
            dma((3,)), dma((3,)), dma((3,)), dma((3,)),
        ],
        compiler_params=pltpu.CompilerParams(
            collective_id=1, has_side_effects=True, vmem_limit_bytes=VMEM_LIMIT
        ),
    )(
        features.reshape(16, TILE, WIDTH), values, weight, bias.reshape(1, WIDTH),
        cotangent.reshape(4, TILE, WIDTH), pulls, rows, picks, counts, pulls,
    )


def hand_over_kernel(*refs):
    into, out_of, sources, targets, held = refs[12], refs[13], refs[:4], refs[4:8], refs[8:12]
    come = [pltpu.make_async_copy(sources[n], held[n], into.at[n]) for n in range(4)]
    go = [pltpu.make_async_copy(held[n], targets[n], out_of.at[n]) for n in range(4)]
    for copy in come:
        copy.start()
    for n in (0, 2, 3, 1):
        come[n].wait()
        go[n].start()
    for copy in go:
        copy.wait()


def hand_over(*arrays):
    hbm = pl.BlockSpec(memory_space=pl.ANY)
    return pl.pallas_call(
        hand_over_kernel,
        name="hand_over",
        out_shape=tuple(jax.ShapeDtypeStruct(array.shape, array.dtype) for array in arrays),
        in_specs=[hbm] * 4,
        out_specs=(hbm,) * 4,
        scratch_shapes=[pltpu.VMEM(array.shape, array.dtype) for array in arrays]
        + [pltpu.SemaphoreType.DMA((4,))] * 2,
        compiler_params=pltpu.CompilerParams(vmem_limit_bytes=VMEM_LIMIT),
    )(*arrays)


def local(
    features, weight, bias, cotangent, tile_vals, tile_rows, tile_pick, tile_count, pull_cols
):
    act, fgrad, wgrad, bgrad = hand_over(*layer(
        features,
        tile_vals.reshape(SECTIONS, SLOTS, TILE, TILE),
        weight,
        bias,
        cotangent,
        tile_rows.reshape(SECTIONS, SLOTS).T,
        tile_pick.reshape(SECTIONS, SLOTS).T,
        tile_count.reshape(1, SECTIONS),
        pull_cols.reshape(SECTIONS, 2).T,
    ))
    return (
        act.reshape(QUARTER, WIDTH),
        fgrad.reshape(QUARTER, WIDTH),
        wgrad.reshape(WIDTH, WIDTH),
        bgrad.reshape(WIDTH),
    )


def solution(mesh):
    in_specs = (
        P("rows", None),
        P(),
        P(),
        P(("rows", "rep"), None),
        P("rows", "rep", None, None, None, None),
        P("rows", "rep", None, None),
        P("rows", "rep", None, None),
        P("rows", "rep", None),
        P("rows", "rep", None, None),
    )
    out_specs = (P(("rows", "rep"), None), P(("rows", "rep"), None), P(), P())
    return jax.shard_map(local, mesh=mesh, in_specs=in_specs, out_specs=out_specs, check_vma=False)
```

```python
import functools

import jax
import jax.numpy as jnp
from jax import lax
from jax.experimental import pallas as pl
from jax.experimental.pallas import tpu as pltpu
from jax.sharding import PartitionSpec as P

MESH = pl.DeviceIdType.MESH
BF = jnp.bfloat16
F32 = jnp.float32
TILE = 128
WIDTH = 256
SECTIONS = 32
SLOTS = 4
QUARTER = 512
ROWS = 2048
VMEM_LIMIT = 60 << 20


class Place:
    def __init__(self):
        rows, rep = lax.axis_index("rows"), lax.axis_index("rep")
        self.yh, x, z = rows // 16, (rows // 4) % 4, rows % 4
        self.x, self.z = x, z
        self.yl, self.core = rep // 2, rep % 2
        self.a = x + self.core * (z - x)
        self.b = z + self.core * (x - z)

    def section(self, yh, a, b):
        x = a + self.core * (b - a)
        z = b + self.core * (a - b)
        return yh * 16 + x * 4 + z

    def a_peer(self, j):
        return (self.section(self.yh, (self.a + j) % 4, self.b), self.yl * 2 + self.core)

    def b_peer(self, j):
        return (self.section(self.yh, self.a, (self.b + j) % 4), self.yl * 2 + self.core)

    def y_peer(self):
        return (self.section(1 - self.yh, self.a, self.b), self.yl * 2 + self.core)

    def near_peer(self, mask):
        yh = (self.yh + mask // 4) % 2
        yl = (self.yl + (mask // 2) % 2) % 2
        core = (self.core + mask % 2) % 2
        rows = lax.axis_index("rows")
        return (yh * 16 + rows % 16, yl * 2 + core)

    def near_id(self):
        return self.yh * 4 + self.yl * 2 + self.core

    def x_peer(self, j):
        rows = lax.axis_index("rows")
        return (self.yh * 16 + (rows + 4 * j) % 16, self.yl * 2 + self.core)

    def z_peer(self, j):
        rows = lax.axis_index("rows")
        return (rows // 4 * 4 + (rows + j) % 4, self.yl * 2 + self.core)


def greet(peers):
    barrier = pltpu.get_barrier_semaphore()
    for peer in peers:
        pl.semaphore_signal(barrier, inc=1, device_id=peer, device_id_type=MESH)
    pl.semaphore_wait(barrier, len(peers))


def remote(src, dst, send, recv, peer):
    return pltpu.make_async_remote_copy(
        src_ref=src, dst_ref=dst, send_sem=send, recv_sem=recv, device_id=peer, device_id_type=MESH
    )


def masked(values, section, picks, counts):
    halves = []
    for p in range(2):
        parts = []
        for t in range(SLOTS):
            keep = jnp.logical_and(picks[t, section] == p, t < counts[0, section])
            scale = jnp.where(keep, jnp.float32(1), jnp.float32(0))
            parts.append(values[section, t] * jnp.full((TILE, TILE), scale, F32).astype(BF))
        halves.append(jnp.concatenate(parts, axis=0))
    return jnp.concatenate(halves, axis=1)


def layer_kernel(
    features, values_hbm, weight_hbm, bias_hbm, cot_hbm, rows_hbm, picks_hbm, counts_hbm, pulls_hbm,
    act_out, fgrad_out, wgrad_out, bgrad_out, *scratch,
):
    dense, scratch = scratch[:8], scratch[8:]
    (values, weight, bias, cotangent, rows, picks, counts, pulls, pull_vec, asked, wants, packed, got, running, last,
     swap_out, from_core, to_near, from_near, agg_all, slope_all, act, back,
     terms, from_b, to_y, from_y, to_a, from_a, held, fgrad,
     w0, n1, s1, w2, s2, w3, s4, wgrad, b1, x1, b2, z1, bgrad,
     load_sem, own_sem, pull_sem, want_sem, act_sem, fgrad_sem, wgrad_sem, bgrad_sem, ask_send, ask_recv,
     fa_send, fa_recv, fr_send, fr_recv, fy_send, fy_recv, fb_send, fb_recv,
     core_send, core_recv, near_send, near_recv,
     gc_send, gc_recv, gn_send, gn_recv, gf_send, gf_recv,
     b_send, b_recv, y_send, y_recv, a_send, a_recv,
     n1_send, n1_recv, w2_send, w2_recv, w3_send, w3_recv, w4_send, w4_recv, w5_send, w5_recv,
     x1_send, x1_recv, z1_send, z1_recv) = scratch
    me = Place()
    fetch = pltpu.make_async_copy(
        features.at[pl.ds((me.yl * 2 + me.core) * 4, 4)], dense[0], own_sem
    )
    fetch.start()
    fetch_pull = pltpu.make_async_copy(pulls_hbm, pull_vec, pull_sem)
    fetch_pull.start()
    loads = [
        pltpu.make_async_copy(src, dst, load_sem.at[n])
        for n, (src, dst) in enumerate([
            (pulls_hbm, pulls), (rows_hbm, rows), (picks_hbm, picks), (counts_hbm, counts),
            (values_hbm, values), (weight_hbm, weight), (bias_hbm, bias), (cot_hbm, cotangent),
        ])
    ]
    for load in loads:
        load.start()
    greet(
        [me.near_peer(m) for m in range(1, 8)]
        + [me.a_peer(j) for j in (1, 2, 3)]
        + [me.b_peer(j) for j in (1, 2, 3)]
    )

    def ask(j):
        return remote(pull_vec, asked.at[j - 1], ask_send.at[j - 1], ask_recv.at[j - 1], me.b_peer(j))

    fetch_pull.wait()
    for j in (1, 2, 3):
        ask(j).start()
    fetch.wait()

    def along(j):
        return remote(dense[0], dense[j], fa_send.at[j - 1], fa_recv.at[j - 1], me.a_peer(j))

    def relay(j):
        half = pl.ds(j // 2 * 2, 2)
        return remote(
            dense[j].at[half], dense[2].at[half], fr_send.at[j // 2], fr_recv.at[j // 2], me.a_peer(j)
        )

    def across(j):
        return remote(dense[j], dense[4 + j], fy_send.at[j], fy_recv.at[j], me.y_peer())

    def give(n, to):
        return remote(
            packed.at[to - 1, n], got.at[to, n], fb_send.at[to - 1, n], fb_recv.at[to - 1, n], me.b_peer(to)
        )

    def block_section(n, b):
        return me.section((me.yh + n // 4) % 2, (me.a + 4 - n % 4) % 4, b)

    for j in (1, 3):
        along(j).start()
    across(0).start()
    loads[0].wait()
    for j in (1, 2, 3):
        ask(j).wait()
        table = pltpu.make_async_copy(asked.at[j - 1], wants.at[j - 1], want_sem)
        table.start()
        table.wait()

    def serve(n):
        column = block_section(n, me.b)
        for source in (1, 3, 2):
            to = 4 - source
            for p in range(2):
                packed[to - 1, n, p] = dense[n][wants[source - 1, p, column]]
            give(n, to).start()
        for p in range(2):
            got[0, n, p] = dense[n][pulls[p, column]]

    serve(0)
    for j in (1, 3):
        along(j).wait_recv()
        relay(j).start()
        across(j).start()
        serve(j)
    for j in (1, 3):
        relay(j).wait_recv()
    across(2).start()
    serve(2)
    for j in (0, 1, 3, 2):
        across(j).wait_recv()
        serve(4 + j)

    for load in loads[1:]:
        load.wait()
    running[128] = jnp.zeros((TILE, WIDTH), F32)

    def forward(step, carry):
        ends = list(carry)
        n = step // 4 * 4 + (step % 4 + (step % 4) // 2 * (5 - 2 * (step % 4)))
        for j in (1, 2, 3):
            give(n, j).wait_recv()
        for source in range(4):
            section = block_section(n, (me.b + 4 - source) % 4)
            block = got[source, n].reshape(2 * TILE, WIDTH)
            sums = jnp.dot(masked(values, section, picks, counts), block, preferred_element_type=F32)
            for t in range(SLOTS):
                row = rows[t, section]
                before = jnp.int32(128)
                slot = (step * 4 + source) * 4 + t
                for r in range(16):
                    before = jnp.where(row == r, ends[r], before)
                    ends[r] = jnp.where(row == r, slot, ends[r])
                running[slot] = sums[t * TILE:(t + 1) * TILE] + running[before]
        return tuple(ends)

    ends = lax.fori_loop(0, 8, forward, (jnp.int32(128),) * 16)
    for r in range(16):
        last[r] = ends[r]

    def part(r):
        return running[last[r]]

    core_peer, near_peer = me.near_peer(1), me.near_peer(2)
    quarters = [(1 - me.yl) * 2, me.yl * 2]

    def swap(n, t):
        return remote(swap_out.at[n, t], from_core.at[n, t], core_send.at[n, t], core_recv.at[n, t], core_peer)

    def over(t):
        return remote(to_near.at[t], from_near.at[t], near_send.at[t], near_recv.at[t], near_peer)

    for n in range(2):
        for t in range(4):
            swap_out[n, t] = part((quarters[n] + 1 - me.core) * 4 + t)
            swap(n, t).start()
    for t in range(4):
        swap(0, t).wait_recv()
        to_near[t] = (part((quarters[0] + me.core) * 4 + t) + from_core[0, t]).astype(BF)
        over(t).start()

    mine = me.yl * 2 + me.core
    yours = (1 - me.yl) * 2 + me.core

    def share_core(t):
        ref = back.at[mine * 4 + t]
        return remote(ref, ref, gc_send.at[t], gc_recv.at[t], core_peer)

    def share_near(t):
        ref = back.at[mine * 4 + t]
        return remote(ref, ref, gn_send.at[t], gn_recv.at[t], near_peer)

    def forward_on(t):
        ref = back.at[yours * 4 + t]
        return remote(ref, ref, gf_send.at[t], gf_recv.at[t], core_peer)

    for t in range(4):
        swap(1, t).wait_recv()
        over(t).wait_recv()
        agg = (part(mine * 4 + t) + from_core[1, t] + from_near[t].astype(F32)).astype(BF)
        agg_all[t * TILE:(t + 1) * TILE] = agg
        pre = jnp.dot(agg, weight[...], preferred_element_type=F32) + bias[...]
        sig = 1.0 / (1.0 + jnp.exp(-pre))
        act[t] = (pre * sig).astype(BF)
        slope = (cotangent[t].astype(F32) * (sig * (1.0 + pre * (1.0 - sig)))).astype(BF)
        slope_all[t * TILE:(t + 1) * TILE] = slope
        back[mine * 4 + t] = lax.dot_general(
            slope, weight[...], (((1,), (1,)), ((), ())), preferred_element_type=F32
        ).astype(BF)
        share_near(t).start()
        share_core(t).start()
    give_act = pltpu.make_async_copy(act, act_out, act_sem)
    give_act.start()

    grad = lax.dot_general(
        agg_all[...], slope_all[...], (((0,), (0,)), ((), ())), preferred_element_type=F32
    )
    bias_sum = jnp.sum(slope_all[...].astype(F32), axis=0, keepdims=True)
    for m in range(8):
        w0[m, :32] = grad[m * 32:(m + 1) * 32]
        w0[m, 32:40] = jnp.broadcast_to(bias_sum, (8, WIDTH))

    def n1_copy(m):
        other = (me.yh + m // 4) % 2 * 4 + (me.yl + m // 2 % 2) % 2 * 2 + (me.core + m % 2) % 2
        return remote(
            w0.at[other], n1.at[me.near_id()], n1_send.at[m - 1], n1_recv.at[m - 1], me.near_peer(m)
        )

    def w2_copy(j):
        return remote(
            s1.at[(me.a + j) % 4], w2.at[me.a], w2_send.at[j - 1], w2_recv.at[j - 1], me.a_peer(j)
        )

    def x1_copy(j):
        return remote(b1, x1.at[me.x], x1_send.at[j - 1], x1_recv.at[j - 1], me.x_peer(j))

    def w3_copy(j):
        return remote(s2, w3.at[me.b], w3_send.at[j - 1], w3_recv.at[j - 1], me.b_peer(j))

    def z1_copy(j):
        return remote(b2, z1.at[me.z], z1_send.at[j - 1], z1_recv.at[j - 1], me.z_peer(j))

    def w4_copy(j):
        return remote(s4.at[me.a], s4.at[me.a], w4_send.at[j - 1], w4_recv.at[j - 1], me.a_peer(j))

    def w5_copy(m):
        ref = wgrad.at[me.near_id()]
        return remote(ref, ref, w5_send.at[m - 1], w5_recv.at[m - 1], me.near_peer(m))

    for m in range(1, 8):
        n1_copy(m).start()
    n1[me.near_id()] = w0[me.near_id()]

    give_bgrad = pltpu.make_async_copy(bgrad, bgrad_out, bgrad_sem)

    def weight_over_a():
        for m in range(1, 8):
            n1_copy(m).wait()
        total = n1[0]
        for m in range(1, 8):
            total = total + n1[m]
        for a in range(4):
            s1[a] = total[a * 8:(a + 1) * 8]
        b1[...] = total[32:40]
        for j in (1, 2, 3):
            w2_copy(j).start()
            x1_copy(j).start()
        w2[me.a] = s1[me.a]
        x1[me.x] = b1[...]

    def weight_over_b():
        for j in (1, 2, 3):
            w2_copy(j).wait()
            x1_copy(j).wait()
        s2[...] = w2[0] + w2[1] + w2[2] + w2[3]
        b2[...] = x1[0] + x1[1] + x1[2] + x1[3]
        for j in (1, 2, 3):
            w3_copy(j).start()
            z1_copy(j).start()
        w3[me.b] = s2[...]
        z1[me.z] = b2[...]

    def weight_back_a():
        for j in (1, 2, 3):
            w3_copy(j).wait()
            z1_copy(j).wait()
        s4[me.a] = w3[0] + w3[1] + w3[2] + w3[3]
        bgrad[...] = (z1[0] + z1[1] + z1[2] + z1[3])[:1]
        give_bgrad.start()
        for j in (1, 2, 3):
            w4_copy(j).start()

    def weight_back_near():
        for j in (1, 2, 3):
            w4_copy(j).wait()
        wgrad[me.near_id()] = s4[...].reshape(32, WIDTH)
        for m in range(1, 8):
            w5_copy(m).start()

    for t in range(4):
        share_near(t).wait_recv()
        forward_on(t).start()
    for t in range(4):
        share_core(t).wait()
        forward_on(t).wait()

    def place(k):
        return (me.yh + 1 + k // 4) % 2, (me.a + 1 + k % 4) % 4

    def send_b(k, j):
        return remote(
            terms.at[j, k], from_b.at[j - 1, k], b_send.at[j - 1, k], b_recv.at[j - 1, k], me.b_peer(j)
        )

    def products(k, j):
        yh, a = place(k)
        section = me.section(yh, a, (me.b + j) % 4)
        sources = jnp.concatenate([back[rows[t, section]] for t in range(SLOTS)], axis=0)
        terms[j, k] = lax.dot_general(
            masked(values, section, picks, counts), sources, (((0,), (0,)), ((), ())),
            preferred_element_type=F32,
        ).astype(BF)

    def contribute(k):
        for j in (1, 3, 2):
            products(k, j)
            send_b(k, j).start()

    def send_y(k):
        return remote(to_y.at[k], from_y.at[k], y_send.at[k], y_recv.at[k], me.y_peer())

    def send_a(k):
        return remote(to_a.at[k], from_a.at[k], a_send.at[k], a_recv.at[k], me.a_peer(1 + k))

    def gather_b(k, q):
        yh, a = place(k)
        section = me.section(yh, a, me.b)
        sums = jnp.zeros((TILE, WIDTH), F32)
        for source in range(4):
            for p in range(2):
                if source == 0:
                    hit, tile = pulls[p, section] == q, terms[0, k, p * TILE:(p + 1) * TILE]
                else:
                    hit = wants[source - 1, p, section] == q
                    tile = from_b[source - 1, k, p * TILE:(p + 1) * TILE]
                sums += tile.astype(F32) * jnp.where(hit, jnp.float32(1), jnp.float32(0))
        return sums

    def arrive_b(k):
        for j in (1, 2, 3):
            send_b(k, j).wait_recv()

    def start(k, carry):
        contribute(k)
        pl.when(k == 2)(weight_over_a)
        return carry

    def other_half(k, carry):
        products(k, 0)
        arrive_b(k)

        def column(q, inner):
            to_y[k, q] = gather_b(k, q).astype(BF)
            return inner

        lax.fori_loop(0, 4, column, 0)
        send_y(k).start()
        contribute(4 + k)
        pl.when(k == 0)(weight_over_b)
        pl.when(k == 2)(weight_back_a)
        return carry

    def this_half(k, carry):
        products(4 + k, 0)
        arrive_b(4 + k)
        send_y(k).wait_recv()

        def column(q, inner):
            sums = gather_b(4 + k, q) + from_y[k, q].astype(F32)
            to_a[k, q] = sums.astype(BF)
            held[q] = sums
            return inner

        lax.fori_loop(0, 4, column, 0)

        @pl.when(k < 3)
        def _():
            send_a(k).start()

        pl.when(k == 0)(weight_back_near)
        return carry

    lax.fori_loop(0, 4, start, 0)
    lax.fori_loop(0, 4, other_half, 0)
    lax.fori_loop(0, 4, this_half, 0)
    for m in range(1, 8):
        w5_copy(m).wait()
    give_wgrad = pltpu.make_async_copy(wgrad, wgrad_out, wgrad_sem)
    give_wgrad.start()
    for k in range(3):
        send_a(k).wait_recv()
    for q in range(4):
        fgrad[q] = held[q] + from_a[0, q].astype(F32) + from_a[1, q].astype(F32) + from_a[2, q].astype(F32)
    give_fgrad = pltpu.make_async_copy(fgrad, fgrad_out, fgrad_sem)
    give_fgrad.start()

    for j in (1, 3):
        along(j).wait_send()
        relay(j).wait_send()
    for j in range(4):
        across(j).wait_send()
        over(j).wait_send()
        share_near(j).wait_send()
        send_y(j).wait_send()
        for n in range(2):
            swap(n, j).wait_send()
    for k in range(3):
        send_a(k).wait_send()

    def drain(n, carry):
        for j in (1, 2, 3):
            give(n, j).wait_send()
            send_b(n, j).wait_send()
        return carry

    lax.fori_loop(0, 8, drain, 0)
    give_act.wait()
    give_bgrad.wait()
    give_wgrad.wait()
    give_fgrad.wait()


def layer(features, values, weight, bias, cotangent, rows, picks, counts, pulls):
    dma = pltpu.SemaphoreType.DMA
    hbm = pl.BlockSpec(memory_space=pl.ANY)
    return pl.pallas_call(
        layer_kernel,
        name="layer",
        out_shape=(
            jax.ShapeDtypeStruct((4, TILE, WIDTH), BF),
            jax.ShapeDtypeStruct((4, TILE, WIDTH), F32),
            jax.ShapeDtypeStruct((8, 32, WIDTH), F32),
            jax.ShapeDtypeStruct((1, WIDTH), F32),
        ),
        in_specs=[hbm] * 9,
        out_specs=(hbm,) * 4,
        scratch_shapes=[
            *[pltpu.VMEM((4, TILE, WIDTH), BF)] * 8,
            pltpu.VMEM((SECTIONS, SLOTS, TILE, TILE), BF),
            pltpu.VMEM((WIDTH, WIDTH), BF),
            pltpu.VMEM((1, WIDTH), F32),
            pltpu.VMEM((4, TILE, WIDTH), BF),
            pltpu.SMEM((SLOTS, SECTIONS), jnp.int32),
            pltpu.SMEM((SLOTS, SECTIONS), jnp.int32),
            pltpu.SMEM((1, SECTIONS), jnp.int32),
            pltpu.SMEM((2, SECTIONS), jnp.int32),
            pltpu.VMEM((2, SECTIONS), jnp.int32),
            pltpu.VMEM((3, 2, SECTIONS), jnp.int32),
            pltpu.SMEM((3, 2, SECTIONS), jnp.int32),
            pltpu.VMEM((3, 8, 2, TILE, WIDTH), BF),
            pltpu.VMEM((4, 8, 2, TILE, WIDTH), BF),
            pltpu.VMEM((129, TILE, WIDTH), F32),
            pltpu.SMEM((16,), jnp.int32),
            pltpu.VMEM((2, 4, TILE, WIDTH), F32),
            pltpu.VMEM((2, 4, TILE, WIDTH), F32),
            pltpu.VMEM((4, TILE, WIDTH), BF),
            pltpu.VMEM((4, TILE, WIDTH), BF),
            pltpu.VMEM((QUARTER, WIDTH), BF),
            pltpu.VMEM((QUARTER, WIDTH), BF),
            pltpu.VMEM((4, TILE, WIDTH), BF),
            pltpu.VMEM((16, TILE, WIDTH), BF),
            pltpu.VMEM((4, 8, 2 * TILE, WIDTH), BF),
            pltpu.VMEM((3, 8, 2 * TILE, WIDTH), BF),
            pltpu.VMEM((4, 4, TILE, WIDTH), BF),
            pltpu.VMEM((4, 4, TILE, WIDTH), BF),
            pltpu.VMEM((4, 4, TILE, WIDTH), BF),
            pltpu.VMEM((3, 4, TILE, WIDTH), BF),
            pltpu.VMEM((4, TILE, WIDTH), F32),
            pltpu.VMEM((4, TILE, WIDTH), F32),
            pltpu.VMEM((8, 40, WIDTH), F32),
            pltpu.VMEM((8, 40, WIDTH), F32),
            pltpu.VMEM((4, 8, WIDTH), F32),
            pltpu.VMEM((4, 8, WIDTH), F32),
            pltpu.VMEM((8, WIDTH), F32),
            pltpu.VMEM((4, 8, WIDTH), F32),
            pltpu.VMEM((4, 8, WIDTH), F32),
            pltpu.VMEM((8, 32, WIDTH), F32),
            pltpu.VMEM((8, WIDTH), F32),
            pltpu.VMEM((4, 8, WIDTH), F32),
            pltpu.VMEM((8, WIDTH), F32),
            pltpu.VMEM((4, 8, WIDTH), F32),
            pltpu.VMEM((1, WIDTH), F32),
            dma((8,)), *[dma] * 7, dma((3,)), dma((3,)),
            dma((3,)), dma((3,)), dma((2,)), dma((2,)), dma((4,)), dma((4,)), dma((3, 8)), dma((3, 8)),
            dma((2, 4)), dma((2, 4)), dma((4,)), dma((4,)),
            dma((4,)), dma((4,)), dma((4,)), dma((4,)), dma((4,)), dma((4,)),
            dma((3, 8)), dma((3, 8)), dma((4,)), dma((4,)), dma((3,)), dma((3,)),
            dma((7,)), dma((7,)), dma((3,)), dma((3,)), dma((3,)), dma((3,)),
            dma((3,)), dma((3,)), dma((7,)), dma((7,)),
            dma((3,)), dma((3,)), dma((3,)), dma((3,)),
        ],
        compiler_params=pltpu.CompilerParams(
            collective_id=1, has_side_effects=True, vmem_limit_bytes=VMEM_LIMIT
        ),
    )(
        features.reshape(16, TILE, WIDTH), values, weight, bias.reshape(1, WIDTH),
        cotangent.reshape(4, TILE, WIDTH), rows, picks, counts, pulls,
    )


def hand_over_kernel(*refs):
    into, out_of, sources, targets, held = refs[12], refs[13], refs[:4], refs[4:8], refs[8:12]
    come = [pltpu.make_async_copy(sources[n], held[n], into.at[n]) for n in range(4)]
    go = [pltpu.make_async_copy(held[n], targets[n], out_of.at[n]) for n in range(4)]
    for copy in come:
        copy.start()
    for n in (0, 2, 3, 1):
        come[n].wait()
        go[n].start()
    for copy in go:
        copy.wait()


def hand_over(*arrays):
    hbm = pl.BlockSpec(memory_space=pl.ANY)
    return pl.pallas_call(
        hand_over_kernel,
        name="hand_over",
        out_shape=tuple(jax.ShapeDtypeStruct(array.shape, array.dtype) for array in arrays),
        in_specs=[hbm] * 4,
        out_specs=(hbm,) * 4,
        scratch_shapes=[pltpu.VMEM(array.shape, array.dtype) for array in arrays]
        + [pltpu.SemaphoreType.DMA((4,))] * 2,
        compiler_params=pltpu.CompilerParams(vmem_limit_bytes=VMEM_LIMIT),
    )(*arrays)


def local(
    features, weight, bias, cotangent, tile_vals, tile_rows, tile_pick, tile_count, pull_cols
):
    act, fgrad, wgrad, bgrad = hand_over(*layer(
        features,
        tile_vals.reshape(SECTIONS, SLOTS, TILE, TILE),
        weight,
        bias,
        cotangent,
        tile_rows.reshape(SECTIONS, SLOTS).T,
        tile_pick.reshape(SECTIONS, SLOTS).T,
        tile_count.reshape(1, SECTIONS),
        pull_cols.reshape(SECTIONS, 2).T,
    ))
    return (
        act.reshape(QUARTER, WIDTH),
        fgrad.reshape(QUARTER, WIDTH),
        wgrad.reshape(WIDTH, WIDTH),
        bgrad.reshape(WIDTH),
    )


def solution(mesh):
    in_specs = (
        P("rows", None),
        P(),
        P(),
        P(("rows", "rep"), None),
        P("rows", "rep", None, None, None, None),
        P("rows", "rep", None, None),
        P("rows", "rep", None, None),
        P("rows", "rep", None),
        P("rows", "rep", None, None),
    )
    out_specs = (P(("rows", "rep"), None), P(("rows", "rep"), None), P(), P())
    return jax.shard_map(local, mesh=mesh, in_specs=in_specs, out_specs=out_specs, check_vma=False)
```

```python
import functools

import jax
import jax.numpy as jnp
from jax import lax
from jax.experimental import pallas as pl
from jax.experimental.pallas import tpu as pltpu
from jax.sharding import PartitionSpec as P

MESH = pl.DeviceIdType.MESH
BF = jnp.bfloat16
F32 = jnp.float32
TILE = 128
WIDTH = 256
SECTIONS = 32
SLOTS = 4
QUARTER = 512
ROWS = 2048
VMEM_LIMIT = 60 << 20


class Place:
    def __init__(self):
        rows, rep = lax.axis_index("rows"), lax.axis_index("rep")
        self.yh, x, z = rows // 16, (rows // 4) % 4, rows % 4
        self.x, self.z = x, z
        self.yl, self.core = rep // 2, rep % 2
        self.a = x + self.core * (z - x)
        self.b = z + self.core * (x - z)

    def section(self, yh, a, b):
        x = a + self.core * (b - a)
        z = b + self.core * (a - b)
        return yh * 16 + x * 4 + z

    def a_peer(self, j):
        return (self.section(self.yh, (self.a + j) % 4, self.b), self.yl * 2 + self.core)

    def b_peer(self, j):
        return (self.section(self.yh, self.a, (self.b + j) % 4), self.yl * 2 + self.core)

    def y_peer(self):
        return (self.section(1 - self.yh, self.a, self.b), self.yl * 2 + self.core)

    def near_peer(self, mask):
        yh = (self.yh + mask // 4) % 2
        yl = (self.yl + (mask // 2) % 2) % 2
        core = (self.core + mask % 2) % 2
        rows = lax.axis_index("rows")
        return (yh * 16 + rows % 16, yl * 2 + core)

    def near_id(self):
        return self.yh * 4 + self.yl * 2 + self.core

    def x_peer(self, j):
        rows = lax.axis_index("rows")
        return (self.yh * 16 + (rows + 4 * j) % 16, self.yl * 2 + self.core)

    def z_peer(self, j):
        rows = lax.axis_index("rows")
        return (rows // 4 * 4 + (rows + j) % 4, self.yl * 2 + self.core)


def greet(peers):
    barrier = pltpu.get_barrier_semaphore()
    for peer in peers:
        pl.semaphore_signal(barrier, inc=1, device_id=peer, device_id_type=MESH)
    pl.semaphore_wait(barrier, len(peers))


def remote(src, dst, send, recv, peer):
    return pltpu.make_async_remote_copy(
        src_ref=src, dst_ref=dst, send_sem=send, recv_sem=recv, device_id=peer, device_id_type=MESH
    )


def masked(values, section, picks, counts):
    halves = []
    for p in range(2):
        parts = []
        for t in range(SLOTS):
            keep = jnp.logical_and(picks[t, section] == p, t < counts[0, section])
            scale = jnp.where(keep, jnp.float32(1), jnp.float32(0))
            parts.append(values[section, t] * jnp.full((TILE, TILE), scale, F32).astype(BF))
        halves.append(jnp.concatenate(parts, axis=0))
    return jnp.concatenate(halves, axis=1)


def layer_kernel(
    features, values_hbm, weight_hbm, bias_hbm, cot_hbm, rows_hbm, picks_hbm, counts_hbm, pulls_hbm,
    act, fgrad, wgrad, bgrad, *scratch,
):
    dense, scratch = scratch[:8], scratch[8:]
    (values, weight, bias, cotangent, rows, picks, counts, pulls, pull_vec, asked, wants, packed, got, running, last,
     swap_out, from_core, to_near, from_near, agg_all, slope_all, back,
     terms, from_b, to_y, from_y, to_a, from_a,
     w0, n1, s1, w2, s2, w3, s4, b1, x1, b2, z1,
     load_sem, own_sem, pull_sem, want_sem, ask_send, ask_recv,
     fa_send, fa_recv, fr_send, fr_recv, fy_send, fy_recv, fb_send, fb_recv,
     core_send, core_recv, near_send, near_recv,
     gc_send, gc_recv, gn_send, gn_recv, gf_send, gf_recv,
     b_send, b_recv, y_send, y_recv, a_send, a_recv,
     n1_send, n1_recv, w2_send, w2_recv, w3_send, w3_recv, w4_send, w4_recv, w5_send, w5_recv,
     x1_send, x1_recv, z1_send, z1_recv) = scratch
    me = Place()
    fetch = pltpu.make_async_copy(
        features.at[pl.ds((me.yl * 2 + me.core) * 4, 4)], dense[0], own_sem
    )
    fetch.start()
    fetch_pull = pltpu.make_async_copy(pulls_hbm, pull_vec, pull_sem)
    fetch_pull.start()
    loads = [
        pltpu.make_async_copy(src, dst, load_sem.at[n])
        for n, (src, dst) in enumerate([
            (pulls_hbm, pulls), (rows_hbm, rows), (picks_hbm, picks), (counts_hbm, counts),
            (values_hbm, values), (weight_hbm, weight), (bias_hbm, bias), (cot_hbm, cotangent),
        ])
    ]
    for load in loads:
        load.start()
    greet(
        [me.near_peer(m) for m in range(1, 8)]
        + [me.a_peer(j) for j in (1, 2, 3)]
        + [me.b_peer(j) for j in (1, 2, 3)]
    )

    def ask(j):
        return remote(pull_vec, asked.at[j - 1], ask_send.at[j - 1], ask_recv.at[j - 1], me.b_peer(j))

    fetch_pull.wait()
    for j in (1, 2, 3):
        ask(j).start()
    fetch.wait()

    def along(j):
        return remote(dense[0], dense[j], fa_send.at[j - 1], fa_recv.at[j - 1], me.a_peer(j))

    def relay(j):
        half = pl.ds(j // 2 * 2, 2)
        return remote(
            dense[j].at[half], dense[2].at[half], fr_send.at[j // 2], fr_recv.at[j // 2], me.a_peer(j)
        )

    def across(j):
        return remote(dense[j], dense[4 + j], fy_send.at[j], fy_recv.at[j], me.y_peer())

    def give(n, to):
        return remote(
            packed.at[to - 1, n], got.at[to, n], fb_send.at[to - 1, n], fb_recv.at[to - 1, n], me.b_peer(to)
        )

    def block_section(n, b):
        return me.section((me.yh + n // 4) % 2, (me.a + 4 - n % 4) % 4, b)

    for j in (1, 3):
        along(j).start()
    across(0).start()
    loads[0].wait()
    for j in (1, 2, 3):
        ask(j).wait()
        table = pltpu.make_async_copy(asked.at[j - 1], wants.at[j - 1], want_sem)
        table.start()
        table.wait()

    def serve(n):
        column = block_section(n, me.b)
        for source in (1, 3, 2):
            to = 4 - source
            for p in range(2):
                packed[to - 1, n, p] = dense[n][wants[source - 1, p, column]]
            give(n, to).start()
        for p in range(2):
            got[0, n, p] = dense[n][pulls[p, column]]

    serve(0)
    for j in (1, 3):
        along(j).wait_recv()
        relay(j).start()
        across(j).start()
        serve(j)
    for j in (1, 3):
        relay(j).wait_recv()
    across(2).start()
    serve(2)
    for j in (0, 1, 3, 2):
        across(j).wait_recv()
        serve(4 + j)

    for load in loads[1:]:
        load.wait()
    running[128] = jnp.zeros((TILE, WIDTH), F32)

    def forward(step, carry):
        ends = list(carry)
        n = step // 4 * 4 + (step % 4 + (step % 4) // 2 * (5 - 2 * (step % 4)))
        for j in (1, 2, 3):
            give(n, j).wait_recv()
        for source in range(4):
            section = block_section(n, (me.b + 4 - source) % 4)
            block = got[source, n].reshape(2 * TILE, WIDTH)
            sums = jnp.dot(masked(values, section, picks, counts), block, preferred_element_type=F32)
            for t in range(SLOTS):
                row = rows[t, section]
                before = jnp.int32(128)
                slot = (step * 4 + source) * 4 + t
                for r in range(16):
                    before = jnp.where(row == r, ends[r], before)
                    ends[r] = jnp.where(row == r, slot, ends[r])
                running[slot] = sums[t * TILE:(t + 1) * TILE] + running[before]
        return tuple(ends)

    ends = lax.fori_loop(0, 8, forward, (jnp.int32(128),) * 16)
    for r in range(16):
        last[r] = ends[r]

    def part(r):
        return running[last[r]]

    core_peer, near_peer = me.near_peer(1), me.near_peer(2)
    quarters = [(1 - me.yl) * 2, me.yl * 2]

    def swap(n, t):
        return remote(swap_out.at[n, t], from_core.at[n, t], core_send.at[n, t], core_recv.at[n, t], core_peer)

    def over(t):
        return remote(to_near.at[t], from_near.at[t], near_send.at[t], near_recv.at[t], near_peer)

    for n in range(2):
        for t in range(4):
            swap_out[n, t] = part((quarters[n] + 1 - me.core) * 4 + t)
            swap(n, t).start()
    for t in range(4):
        swap(0, t).wait_recv()
        to_near[t] = (part((quarters[0] + me.core) * 4 + t) + from_core[0, t]).astype(BF)
        over(t).start()

    mine = me.yl * 2 + me.core
    yours = (1 - me.yl) * 2 + me.core

    def share_core(t):
        ref = back.at[mine * 4 + t]
        return remote(ref, ref, gc_send.at[t], gc_recv.at[t], core_peer)

    def share_near(t):
        ref = back.at[mine * 4 + t]
        return remote(ref, ref, gn_send.at[t], gn_recv.at[t], near_peer)

    def forward_on(t):
        ref = back.at[yours * 4 + t]
        return remote(ref, ref, gf_send.at[t], gf_recv.at[t], core_peer)

    for t in range(4):
        swap(1, t).wait_recv()
        over(t).wait_recv()
        agg = (part(mine * 4 + t) + from_core[1, t] + from_near[t].astype(F32)).astype(BF)
        agg_all[t * TILE:(t + 1) * TILE] = agg
        pre = jnp.dot(agg, weight[...], preferred_element_type=F32) + bias[...]
        sig = 1.0 / (1.0 + jnp.exp(-pre))
        act[t] = (pre * sig).astype(BF)
        slope = (cotangent[t].astype(F32) * (sig * (1.0 + pre * (1.0 - sig)))).astype(BF)
        slope_all[t * TILE:(t + 1) * TILE] = slope
        back[mine * 4 + t] = lax.dot_general(
            slope, weight[...], (((1,), (1,)), ((), ())), preferred_element_type=F32
        ).astype(BF)
        share_near(t).start()
        share_core(t).start()

    grad = lax.dot_general(
        agg_all[...], slope_all[...], (((0,), (0,)), ((), ())), preferred_element_type=F32
    )
    bias_sum = jnp.sum(slope_all[...].astype(F32), axis=0, keepdims=True)
    for m in range(8):
        w0[m, :32] = grad[m * 32:(m + 1) * 32]
        w0[m, 32:40] = jnp.broadcast_to(bias_sum, (8, WIDTH))

    def n1_copy(m):
        other = (me.yh + m // 4) % 2 * 4 + (me.yl + m // 2 % 2) % 2 * 2 + (me.core + m % 2) % 2
        return remote(
            w0.at[other], n1.at[me.near_id()], n1_send.at[m - 1], n1_recv.at[m - 1], me.near_peer(m)
        )

    def w2_copy(j):
        return remote(
            s1.at[(me.a + j) % 4], w2.at[me.a], w2_send.at[j - 1], w2_recv.at[j - 1], me.a_peer(j)
        )

    def x1_copy(j):
        return remote(b1, x1.at[me.x], x1_send.at[j - 1], x1_recv.at[j - 1], me.x_peer(j))

    def w3_copy(j):
        return remote(s2, w3.at[me.b], w3_send.at[j - 1], w3_recv.at[j - 1], me.b_peer(j))

    def z1_copy(j):
        return remote(b2, z1.at[me.z], z1_send.at[j - 1], z1_recv.at[j - 1], me.z_peer(j))

    def w4_copy(j):
        return remote(s4.at[me.a], s4.at[me.a], w4_send.at[j - 1], w4_recv.at[j - 1], me.a_peer(j))

    def w5_copy(m):
        ref = wgrad.at[me.near_id()]
        return remote(ref, ref, w5_send.at[m - 1], w5_recv.at[m - 1], me.near_peer(m))

    for m in range(1, 8):
        n1_copy(m).start()
    n1[me.near_id()] = w0[me.near_id()]

    def weight_over_a():
        for m in range(1, 8):
            n1_copy(m).wait()
        total = n1[0]
        for m in range(1, 8):
            total = total + n1[m]
        for a in range(4):
            s1[a] = total[a * 8:(a + 1) * 8]
        b1[...] = total[32:40]
        for j in (1, 2, 3):
            w2_copy(j).start()
            x1_copy(j).start()
        w2[me.a] = s1[me.a]
        x1[me.x] = b1[...]

    def weight_over_b():
        for j in (1, 2, 3):
            w2_copy(j).wait()
            x1_copy(j).wait()
        s2[...] = w2[0] + w2[1] + w2[2] + w2[3]
        b2[...] = x1[0] + x1[1] + x1[2] + x1[3]
        for j in (1, 2, 3):
            w3_copy(j).start()
            z1_copy(j).start()
        w3[me.b] = s2[...]
        z1[me.z] = b2[...]

    def weight_back_a():
        for j in (1, 2, 3):
            w3_copy(j).wait()
            z1_copy(j).wait()
        s4[me.a] = w3[0] + w3[1] + w3[2] + w3[3]
        bgrad[...] = (z1[0] + z1[1] + z1[2] + z1[3])[:1]
        for j in (1, 2, 3):
            w4_copy(j).start()

    def weight_back_near():
        for j in (1, 2, 3):
            w4_copy(j).wait()
        wgrad[me.near_id()] = s4[...].reshape(32, WIDTH)
        for m in range(1, 8):
            w5_copy(m).start()

    for t in range(4):
        share_near(t).wait_recv()
        forward_on(t).start()
    for t in range(4):
        share_core(t).wait()
        forward_on(t).wait()

    def step_a(k):
        return 2 - k + k // 2 * 3 - k // 3 * 2

    def place(k):
        return (me.yh + 1 + k // 4) % 2, (me.a + step_a(k % 4)) % 4

    def send_b(k, j):
        return remote(
            terms.at[j, k], from_b.at[j - 1, k], b_send.at[j - 1, k], b_recv.at[j - 1, k], me.b_peer(j)
        )

    def products(k, j):
        yh, a = place(k)
        section = me.section(yh, a, (me.b + j) % 4)
        sources = jnp.concatenate([back[rows[t, section]] for t in range(SLOTS)], axis=0)
        terms[j, k] = lax.dot_general(
            masked(values, section, picks, counts), sources, (((0,), (0,)), ((), ())),
            preferred_element_type=F32,
        ).astype(BF)

    def contribute(k):
        for j in (1, 3, 2):
            products(k, j)
            send_b(k, j).start()

    def send_y(k):
        return remote(to_y.at[k], from_y.at[k], y_send.at[k], y_recv.at[k], me.y_peer())

    def send_a(k):
        return remote(to_a.at[k], from_a.at[k], a_send.at[k], a_recv.at[k], me.a_peer(step_a(k)))

    def gather_b(k, q):
        yh, a = place(k)
        section = me.section(yh, a, me.b)
        sums = jnp.zeros((TILE, WIDTH), F32)
        for source in range(4):
            for p in range(2):
                if source == 0:
                    hit, tile = pulls[p, section] == q, terms[0, k, p * TILE:(p + 1) * TILE]
                else:
                    hit = wants[source - 1, p, section] == q
                    tile = from_b[source - 1, k, p * TILE:(p + 1) * TILE]
                sums += tile.astype(F32) * jnp.where(hit, jnp.float32(1), jnp.float32(0))
        return sums

    def arrive_b(k):
        for j in (1, 2, 3):
            send_b(k, j).wait_recv()

    def start(k, carry):
        contribute(k)
        pl.when(k == 2)(weight_over_a)
        return carry

    def other_half(k, carry):
        contribute(4 + k)
        products(k, 0)
        arrive_b(k)

        def column(q, inner):
            to_y[k, q] = gather_b(k, q).astype(BF)
            return inner

        lax.fori_loop(0, 4, column, 0)
        send_y(k).start()
        pl.when(k == 0)(weight_over_b)
        pl.when(k == 2)(weight_back_a)
        return carry

    def this_half(k, carry):
        products(4 + k, 0)
        arrive_b(4 + k)
        send_y(k).wait_recv()

        def column(q, inner):
            to_a[k, q] = (gather_b(4 + k, q) + from_y[k, q].astype(F32)).astype(BF)
            return inner

        lax.fori_loop(0, 4, column, 0)
        send_a(k).start()
        pl.when(k == 0)(weight_back_near)
        return carry

    lax.fori_loop(0, 4, start, 0)
    lax.fori_loop(0, 4, other_half, 0)
    lax.fori_loop(0, 3, this_half, 0)
    products(7, 0)
    arrive_b(7)
    send_y(3).wait_recv()
    for k in range(3):
        send_a(k).wait_recv()

    def own(q, carry):
        fgrad[q] = gather_b(7, q) + sum(
            (ref[n, q].astype(F32) for ref, n in ((from_y, 3), (from_a, 0), (from_a, 1), (from_a, 2))),
            jnp.zeros((TILE, WIDTH), F32),
        )
        return carry

    lax.fori_loop(0, 4, own, 0)
    for m in range(1, 8):
        w5_copy(m).wait()

    for j in (1, 3):
        along(j).wait_send()
        relay(j).wait_send()
    for j in range(4):
        across(j).wait_send()
        over(j).wait_send()
        share_near(j).wait_send()
        send_y(j).wait_send()
        for n in range(2):
            swap(n, j).wait_send()
    for k in range(3):
        send_a(k).wait_send()

    def drain(n, carry):
        for j in (1, 2, 3):
            give(n, j).wait_send()
            send_b(n, j).wait_send()
        return carry

    lax.fori_loop(0, 8, drain, 0)


def layer(features, values, weight, bias, cotangent, rows, picks, counts, pulls):
    dma = pltpu.SemaphoreType.DMA
    hbm = pl.BlockSpec(memory_space=pl.ANY)
    return pl.pallas_call(
        layer_kernel,
        name="layer",
        out_shape=(
            pltpu.VMEM((4, TILE, WIDTH), BF),
            pltpu.VMEM((4, TILE, WIDTH), F32),
            pltpu.VMEM((8, 32, WIDTH), F32),
            pltpu.VMEM((1, WIDTH), F32),
        ),
        in_specs=[hbm] * 9,
        out_specs=(pl.BlockSpec(memory_space=pltpu.VMEM),) * 4,
        scratch_shapes=[
            *[pltpu.VMEM((4, TILE, WIDTH), BF)] * 8,
            pltpu.VMEM((SECTIONS, SLOTS, TILE, TILE), BF),
            pltpu.VMEM((WIDTH, WIDTH), BF),
            pltpu.VMEM((1, WIDTH), F32),
            pltpu.VMEM((4, TILE, WIDTH), BF),
            pltpu.SMEM((SLOTS, SECTIONS), jnp.int32),
            pltpu.SMEM((SLOTS, SECTIONS), jnp.int32),
            pltpu.SMEM((1, SECTIONS), jnp.int32),
            pltpu.SMEM((2, SECTIONS), jnp.int32),
            pltpu.VMEM((2, SECTIONS), jnp.int32),
            pltpu.VMEM((3, 2, SECTIONS), jnp.int32),
            pltpu.SMEM((3, 2, SECTIONS), jnp.int32),
            pltpu.VMEM((3, 8, 2, TILE, WIDTH), BF),
            pltpu.VMEM((4, 8, 2, TILE, WIDTH), BF),
            pltpu.VMEM((129, TILE, WIDTH), F32),
            pltpu.SMEM((16,), jnp.int32),
            pltpu.VMEM((2, 4, TILE, WIDTH), F32),
            pltpu.VMEM((2, 4, TILE, WIDTH), F32),
            pltpu.VMEM((4, TILE, WIDTH), BF),
            pltpu.VMEM((4, TILE, WIDTH), BF),
            pltpu.VMEM((QUARTER, WIDTH), BF),
            pltpu.VMEM((QUARTER, WIDTH), BF),
            pltpu.VMEM((16, TILE, WIDTH), BF),
            pltpu.VMEM((4, 8, 2 * TILE, WIDTH), BF),
            pltpu.VMEM((3, 8, 2 * TILE, WIDTH), BF),
            pltpu.VMEM((4, 4, TILE, WIDTH), BF),
            pltpu.VMEM((4, 4, TILE, WIDTH), BF),
            pltpu.VMEM((4, 4, TILE, WIDTH), BF),
            pltpu.VMEM((3, 4, TILE, WIDTH), BF),
            pltpu.VMEM((8, 40, WIDTH), F32),
            pltpu.VMEM((8, 40, WIDTH), F32),
            pltpu.VMEM((4, 8, WIDTH), F32),
            pltpu.VMEM((4, 8, WIDTH), F32),
            pltpu.VMEM((8, WIDTH), F32),
            pltpu.VMEM((4, 8, WIDTH), F32),
            pltpu.VMEM((4, 8, WIDTH), F32),
            pltpu.VMEM((8, WIDTH), F32),
            pltpu.VMEM((4, 8, WIDTH), F32),
            pltpu.VMEM((8, WIDTH), F32),
            pltpu.VMEM((4, 8, WIDTH), F32),
            dma((8,)), *[dma] * 3, dma((3,)), dma((3,)),
            dma((3,)), dma((3,)), dma((2,)), dma((2,)), dma((4,)), dma((4,)), dma((3, 8)), dma((3, 8)),
            dma((2, 4)), dma((2, 4)), dma((4,)), dma((4,)),
            dma((4,)), dma((4,)), dma((4,)), dma((4,)), dma((4,)), dma((4,)),
            dma((3, 8)), dma((3, 8)), dma((4,)), dma((4,)), dma((3,)), dma((3,)),
            dma((7,)), dma((7,)), dma((3,)), dma((3,)), dma((3,)), dma((3,)),
            dma((3,)), dma((3,)), dma((7,)), dma((7,)),
            dma((3,)), dma((3,)), dma((3,)), dma((3,)),
        ],
        compiler_params=pltpu.CompilerParams(
            collective_id=1, has_side_effects=True, vmem_limit_bytes=VMEM_LIMIT
        ),
    )(
        features.reshape(16, TILE, WIDTH), values, weight, bias.reshape(1, WIDTH),
        cotangent.reshape(4, TILE, WIDTH), rows, picks, counts, pulls,
    )


def hand_over_kernel(*refs):
    sems = refs[8]
    copies = [pltpu.make_async_copy(refs[n], refs[4 + n], sems.at[n]) for n in range(4)]
    for copy in copies:
        copy.start()
    for copy in copies:
        copy.wait()


def hand_over(*arrays):
    hbm, vmem = pl.BlockSpec(memory_space=pl.ANY), pl.BlockSpec(memory_space=pltpu.VMEM)
    return pl.pallas_call(
        hand_over_kernel,
        name="hand_over",
        out_shape=tuple(jax.ShapeDtypeStruct(array.shape, array.dtype) for array in arrays),
        in_specs=[vmem] * 4,
        out_specs=(hbm,) * 4,
        scratch_shapes=[pltpu.SemaphoreType.DMA((4,))],
        compiler_params=pltpu.CompilerParams(vmem_limit_bytes=4 << 20),
    )(*arrays)


def local(
    features, weight, bias, cotangent, tile_vals, tile_rows, tile_pick, tile_count, pull_cols
):
    act, fgrad, wgrad, bgrad = hand_over(*layer(
        features,
        tile_vals.reshape(SECTIONS, SLOTS, TILE, TILE),
        weight,
        bias,
        cotangent,
        tile_rows.reshape(SECTIONS, SLOTS).T,
        tile_pick.reshape(SECTIONS, SLOTS).T,
        tile_count.reshape(1, SECTIONS),
        pull_cols.reshape(SECTIONS, 2).T,
    ))
    return (
        act.reshape(QUARTER, WIDTH),
        fgrad.reshape(QUARTER, WIDTH),
        wgrad.reshape(WIDTH, WIDTH),
        bgrad.reshape(WIDTH),
    )


def solution(mesh):
    in_specs = (
        P("rows", None),
        P(),
        P(),
        P(("rows", "rep"), None),
        P("rows", "rep", None, None, None, None),
        P("rows", "rep", None, None),
        P("rows", "rep", None, None),
        P("rows", "rep", None),
        P("rows", "rep", None, None),
    )
    out_specs = (P(("rows", "rep"), None), P(("rows", "rep"), None), P(), P())
    return jax.shard_map(local, mesh=mesh, in_specs=in_specs, out_specs=out_specs, check_vma=False)
```

```python
import functools

import jax
import jax.numpy as jnp
from jax import lax
from jax.experimental import pallas as pl
from jax.experimental.pallas import tpu as pltpu
from jax.sharding import PartitionSpec as P

MESH = pl.DeviceIdType.MESH
BF = jnp.bfloat16
F32 = jnp.float32
TILE = 128
WIDTH = 256
SECTIONS = 32
SLOTS = 4
QUARTER = 512
ROWS = 2048
VMEM_LIMIT = 60 << 20


class Place:
    def __init__(self):
        rows, rep = lax.axis_index("rows"), lax.axis_index("rep")
        self.yh, x, z = rows // 16, (rows // 4) % 4, rows % 4
        self.x, self.z = x, z
        self.yl, self.core = rep // 2, rep % 2
        self.a = x + self.core * (z - x)
        self.b = z + self.core * (x - z)

    def section(self, yh, a, b):
        x = a + self.core * (b - a)
        z = b + self.core * (a - b)
        return yh * 16 + x * 4 + z

    def a_peer(self, j):
        return (self.section(self.yh, (self.a + j) % 4, self.b), self.yl * 2 + self.core)

    def b_peer(self, j):
        return (self.section(self.yh, self.a, (self.b + j) % 4), self.yl * 2 + self.core)

    def y_peer(self):
        return (self.section(1 - self.yh, self.a, self.b), self.yl * 2 + self.core)

    def near_peer(self, mask):
        yh = (self.yh + mask // 4) % 2
        yl = (self.yl + (mask // 2) % 2) % 2
        core = (self.core + mask % 2) % 2
        rows = lax.axis_index("rows")
        return (yh * 16 + rows % 16, yl * 2 + core)

    def near_id(self):
        return self.yh * 4 + self.yl * 2 + self.core

    def x_peer(self, j):
        rows = lax.axis_index("rows")
        return (self.yh * 16 + (rows + 4 * j) % 16, self.yl * 2 + self.core)

    def z_peer(self, j):
        rows = lax.axis_index("rows")
        return (rows // 4 * 4 + (rows + j) % 4, self.yl * 2 + self.core)


def greet(peers):
    barrier = pltpu.get_barrier_semaphore()
    for peer in peers:
        pl.semaphore_signal(barrier, inc=1, device_id=peer, device_id_type=MESH)
    pl.semaphore_wait(barrier, len(peers))


def remote(src, dst, send, recv, peer):
    return pltpu.make_async_remote_copy(
        src_ref=src, dst_ref=dst, send_sem=send, recv_sem=recv, device_id=peer, device_id_type=MESH
    )


def masked(values, section, picks, counts):
    halves = []
    for p in range(2):
        parts = []
        for t in range(SLOTS):
            keep = jnp.logical_and(picks[t, section] == p, t < counts[0, section])
            scale = jnp.where(keep, jnp.float32(1), jnp.float32(0))
            parts.append(values[section, t] * jnp.full((TILE, TILE), scale, F32).astype(BF))
        halves.append(jnp.concatenate(parts, axis=0))
    return jnp.concatenate(halves, axis=1)


def layer_kernel(
    features, values_hbm, weight_hbm, bias_hbm, cot_hbm, rows_hbm, picks_hbm, counts_hbm, pulls_hbm,
    act, fgrad, wgrad, bgrad, *scratch,
):
    dense, scratch = scratch[:8], scratch[8:]
    (values, weight, bias, cotangent, rows, picks, counts, pulls, pull_vec, asked, wants, packed, got, running, last,
     swap_out, from_core, to_near, from_near, agg_all, slope_all, back,
     terms, from_b, to_y, from_y, to_a, from_a,
     w0, n1, s1, w2, s2, w3, s4, b1, x1, b2, z1,
     load_sem, own_sem, pull_sem, want_sem, ask_send, ask_recv,
     fa_send, fa_recv, fr_send, fr_recv, fy_send, fy_recv, fb_send, fb_recv,
     core_send, core_recv, near_send, near_recv,
     gc_send, gc_recv, gn_send, gn_recv, gf_send, gf_recv,
     b_send, b_recv, y_send, y_recv, a_send, a_recv,
     n1_send, n1_recv, w2_send, w2_recv, w3_send, w3_recv, w4_send, w4_recv, w5_send, w5_recv,
     x1_send, x1_recv, z1_send, z1_recv) = scratch
    me = Place()
    fetch = pltpu.make_async_copy(
        features.at[pl.ds((me.yl * 2 + me.core) * 4, 4)], dense[0], own_sem
    )
    fetch.start()
    fetch_pull = pltpu.make_async_copy(pulls_hbm, pull_vec, pull_sem)
    fetch_pull.start()
    loads = [
        pltpu.make_async_copy(src, dst, load_sem.at[n])
        for n, (src, dst) in enumerate([
            (pulls_hbm, pulls), (rows_hbm, rows), (picks_hbm, picks), (counts_hbm, counts),
            (values_hbm, values), (weight_hbm, weight), (bias_hbm, bias), (cot_hbm, cotangent),
        ])
    ]
    for load in loads:
        load.start()
    greet(
        [me.near_peer(m) for m in range(1, 8)]
        + [me.a_peer(j) for j in (1, 2, 3)]
        + [me.b_peer(j) for j in (1, 2, 3)]
    )

    def ask(j):
        return remote(pull_vec, asked.at[j - 1], ask_send.at[j - 1], ask_recv.at[j - 1], me.b_peer(j))

    fetch_pull.wait()
    for j in (1, 2, 3):
        ask(j).start()
    fetch.wait()

    def along(j):
        return remote(dense[0], dense[j], fa_send.at[j - 1], fa_recv.at[j - 1], me.a_peer(j))

    def relay(j):
        half = pl.ds(j // 2 * 2, 2)
        return remote(
            dense[j].at[half], dense[2].at[half], fr_send.at[j // 2], fr_recv.at[j // 2], me.a_peer(j)
        )

    def across(j):
        return remote(dense[j], dense[4 + j], fy_send.at[j], fy_recv.at[j], me.y_peer())

    def give(n, to):
        return remote(
            packed.at[to - 1, n], got.at[to, n], fb_send.at[to - 1, n], fb_recv.at[to - 1, n], me.b_peer(to)
        )

    def block_section(n, b):
        return me.section((me.yh + n // 4) % 2, (me.a + 4 - n % 4) % 4, b)

    for j in (1, 3):
        along(j).start()
    across(0).start()
    loads[0].wait()
    for j in (1, 2, 3):
        ask(j).wait()
        table = pltpu.make_async_copy(asked.at[j - 1], wants.at[j - 1], want_sem)
        table.start()
        table.wait()

    def serve(n):
        column = block_section(n, me.b)
        for source in (1, 3, 2):
            to = 4 - source
            for p in range(2):
                packed[to - 1, n, p] = dense[n][wants[source - 1, p, column]]
            give(n, to).start()
        for p in range(2):
            got[0, n, p] = dense[n][pulls[p, column]]

    serve(0)
    for j in (1, 3):
        along(j).wait_recv()
        relay(j).start()
        across(j).start()
    for j in (1, 3):
        serve(j)
    for j in (1, 3):
        relay(j).wait_recv()
    across(2).start()
    serve(2)
    for j in (0, 1, 3, 2):
        across(j).wait_recv()
        serve(4 + j)

    for load in loads[1:]:
        load.wait()
    running[128] = jnp.zeros((TILE, WIDTH), F32)

    def forward(step, carry):
        ends = list(carry)
        n = step // 4 * 4 + (step % 4 + (step % 4) // 2 * (5 - 2 * (step % 4)))
        for j in (1, 2, 3):
            give(n, j).wait_recv()
        for source in range(4):
            section = block_section(n, (me.b + 4 - source) % 4)
            block = got[source, n].reshape(2 * TILE, WIDTH)
            sums = jnp.dot(masked(values, section, picks, counts), block, preferred_element_type=F32)
            for t in range(SLOTS):
                row = rows[t, section]
                before = jnp.int32(128)
                slot = (step * 4 + source) * 4 + t
                for r in range(16):
                    before = jnp.where(row == r, ends[r], before)
                    ends[r] = jnp.where(row == r, slot, ends[r])
                running[slot] = sums[t * TILE:(t + 1) * TILE] + running[before]
        return tuple(ends)

    ends = lax.fori_loop(0, 8, forward, (jnp.int32(128),) * 16)
    for r in range(16):
        last[r] = ends[r]

    def part(r):
        return running[last[r]]

    core_peer, near_peer = me.near_peer(1), me.near_peer(2)
    quarters = [(1 - me.yl) * 2, me.yl * 2]

    def swap(n, t):
        return remote(swap_out.at[n, t], from_core.at[n, t], core_send.at[n, t], core_recv.at[n, t], core_peer)

    def over(t):
        return remote(to_near.at[t], from_near.at[t], near_send.at[t], near_recv.at[t], near_peer)

    def swap_start(n, t):
        swap_out[n, t] = part((quarters[n] + 1 - me.core) * 4 + t)
        swap(n, t).start()

    for t in range(4):
        swap_start(0, t)
    for t in range(4):
        swap(0, t).wait_recv()
        to_near[t] = (part((quarters[0] + me.core) * 4 + t) + from_core[0, t]).astype(BF)
        over(t).start()
    for t in range(4):
        swap_start(1, t)

    mine = me.yl * 2 + me.core
    yours = (1 - me.yl) * 2 + me.core

    def share_core(t):
        ref = back.at[mine * 4 + t]
        return remote(ref, ref, gc_send.at[t], gc_recv.at[t], core_peer)

    def share_near(t):
        ref = back.at[mine * 4 + t]
        return remote(ref, ref, gn_send.at[t], gn_recv.at[t], near_peer)

    def forward_on(t):
        ref = back.at[yours * 4 + t]
        return remote(ref, ref, gf_send.at[t], gf_recv.at[t], core_peer)

    for t in range(4):
        swap(1, t).wait_recv()
        over(t).wait_recv()
        agg = (part(mine * 4 + t) + from_core[1, t] + from_near[t].astype(F32)).astype(BF)
        agg_all[t * TILE:(t + 1) * TILE] = agg
        pre = jnp.dot(agg, weight[...], preferred_element_type=F32) + bias[...]
        sig = 1.0 / (1.0 + jnp.exp(-pre))
        act[t] = (pre * sig).astype(BF)
        slope = (cotangent[t].astype(F32) * (sig * (1.0 + pre * (1.0 - sig)))).astype(BF)
        slope_all[t * TILE:(t + 1) * TILE] = slope
        back[mine * 4 + t] = lax.dot_general(
            slope, weight[...], (((1,), (1,)), ((), ())), preferred_element_type=F32
        ).astype(BF)
        share_near(t).start()
        share_core(t).start()

    grad = lax.dot_general(
        agg_all[...], slope_all[...], (((0,), (0,)), ((), ())), preferred_element_type=F32
    )
    bias_sum = jnp.sum(slope_all[...].astype(F32), axis=0, keepdims=True)
    for m in range(8):
        w0[m, :32] = grad[m * 32:(m + 1) * 32]
        w0[m, 32:40] = jnp.broadcast_to(bias_sum, (8, WIDTH))

    def n1_copy(m):
        other = (me.yh + m // 4) % 2 * 4 + (me.yl + m // 2 % 2) % 2 * 2 + (me.core + m % 2) % 2
        return remote(
            w0.at[other], n1.at[me.near_id()], n1_send.at[m - 1], n1_recv.at[m - 1], me.near_peer(m)
        )

    def w2_copy(j):
        return remote(
            s1.at[(me.a + j) % 4], w2.at[me.a], w2_send.at[j - 1], w2_recv.at[j - 1], me.a_peer(j)
        )

    def x1_copy(j):
        return remote(b1, x1.at[me.x], x1_send.at[j - 1], x1_recv.at[j - 1], me.x_peer(j))

    def w3_copy(j):
        return remote(s2, w3.at[me.b], w3_send.at[j - 1], w3_recv.at[j - 1], me.b_peer(j))

    def z1_copy(j):
        return remote(b2, z1.at[me.z], z1_send.at[j - 1], z1_recv.at[j - 1], me.z_peer(j))

    def w4_copy(j):
        return remote(s4.at[me.a], s4.at[me.a], w4_send.at[j - 1], w4_recv.at[j - 1], me.a_peer(j))

    def w5_copy(m):
        ref = wgrad.at[me.near_id()]
        return remote(ref, ref, w5_send.at[m - 1], w5_recv.at[m - 1], me.near_peer(m))

    for m in range(1, 8):
        n1_copy(m).start()
    n1[me.near_id()] = w0[me.near_id()]

    def weight_over_a():
        for m in range(1, 8):
            n1_copy(m).wait()
        total = n1[0]
        for m in range(1, 8):
            total = total + n1[m]
        for a in range(4):
            s1[a] = total[a * 8:(a + 1) * 8]
        b1[...] = total[32:40]
        for j in (1, 2, 3):
            w2_copy(j).start()
            x1_copy(j).start()
        w2[me.a] = s1[me.a]
        x1[me.x] = b1[...]

    def weight_over_b():
        for j in (1, 2, 3):
            w2_copy(j).wait()
            x1_copy(j).wait()
        s2[...] = w2[0] + w2[1] + w2[2] + w2[3]
        b2[...] = x1[0] + x1[1] + x1[2] + x1[3]
        for j in (1, 2, 3):
            w3_copy(j).start()
            z1_copy(j).start()
        w3[me.b] = s2[...]
        z1[me.z] = b2[...]

    def weight_back_a():
        for j in (1, 2, 3):
            w3_copy(j).wait()
            z1_copy(j).wait()
        s4[me.a] = w3[0] + w3[1] + w3[2] + w3[3]
        bgrad[...] = (z1[0] + z1[1] + z1[2] + z1[3])[:1]
        for j in (1, 2, 3):
            w4_copy(j).start()

    def weight_back_near():
        for j in (1, 2, 3):
            w4_copy(j).wait()
        wgrad[me.near_id()] = s4[...].reshape(32, WIDTH)
        for m in range(1, 8):
            w5_copy(m).start()

    for t in range(4):
        share_near(t).wait_recv()
        forward_on(t).start()
    for t in range(4):
        share_core(t).wait()
        forward_on(t).wait()

    def step_a(k):
        return 2 - k + k // 2 * 3 - k // 3 * 2

    def place(k):
        return (me.yh + 1 + k // 4) % 2, (me.a + step_a(k % 4)) % 4

    def send_b(k, j):
        return remote(
            terms.at[j, k], from_b.at[j - 1, k], b_send.at[j - 1, k], b_recv.at[j - 1, k], me.b_peer(j)
        )

    def products(k, j):
        yh, a = place(k)
        section = me.section(yh, a, (me.b + j) % 4)
        sources = jnp.concatenate([back[rows[t, section]] for t in range(SLOTS)], axis=0)
        terms[j, k] = lax.dot_general(
            masked(values, section, picks, counts), sources, (((0,), (0,)), ((), ())),
            preferred_element_type=F32,
        ).astype(BF)

    def contribute(k):
        for j in (1, 3, 2):
            products(k, j)
            send_b(k, j).start()

    def send_y(k):
        return remote(to_y.at[k], from_y.at[k], y_send.at[k], y_recv.at[k], me.y_peer())

    def send_a(k):
        return remote(to_a.at[k], from_a.at[k], a_send.at[k], a_recv.at[k], me.a_peer(step_a(k)))

    def gather_b(k, q):
        yh, a = place(k)
        section = me.section(yh, a, me.b)
        sums = jnp.zeros((TILE, WIDTH), F32)
        for source in range(4):
            for p in range(2):
                if source == 0:
                    hit, tile = pulls[p, section] == q, terms[0, k, p * TILE:(p + 1) * TILE]
                else:
                    hit = wants[source - 1, p, section] == q
                    tile = from_b[source - 1, k, p * TILE:(p + 1) * TILE]
                sums += tile.astype(F32) * jnp.where(hit, jnp.float32(1), jnp.float32(0))
        return sums

    def arrive_b(k):
        for j in (1, 2, 3):
            send_b(k, j).wait_recv()

    def start(k, carry):
        contribute(k)
        pl.when(k == 2)(weight_over_a)
        return carry

    def other_half(k, carry):
        contribute(4 + k)
        products(k, 0)
        arrive_b(k)

        def column(q, inner):
            to_y[k, q] = gather_b(k, q).astype(BF)
            return inner

        lax.fori_loop(0, 4, column, 0)
        send_y(k).start()
        pl.when(k == 0)(weight_over_b)
        pl.when(k == 2)(weight_back_a)
        return carry

    def this_half(k, carry):
        products(4 + k, 0)
        arrive_b(4 + k)
        send_y(k).wait_recv()

        def column(q, inner):
            to_a[k, q] = (gather_b(4 + k, q) + from_y[k, q].astype(F32)).astype(BF)
            return inner

        lax.fori_loop(0, 4, column, 0)
        send_a(k).start()
        pl.when(k == 0)(weight_back_near)
        return carry

    lax.fori_loop(0, 4, start, 0)
    lax.fori_loop(0, 4, other_half, 0)
    lax.fori_loop(0, 3, this_half, 0)
    products(7, 0)
    arrive_b(7)
    send_y(3).wait_recv()
    for k in range(3):
        send_a(k).wait_recv()

    def own(q, carry):
        fgrad[q] = gather_b(7, q) + sum(
            (ref[n, q].astype(F32) for ref, n in ((from_y, 3), (from_a, 0), (from_a, 1), (from_a, 2))),
            jnp.zeros((TILE, WIDTH), F32),
        )
        return carry

    lax.fori_loop(0, 4, own, 0)
    for m in range(1, 8):
        w5_copy(m).wait()

    for j in (1, 3):
        along(j).wait_send()
        relay(j).wait_send()
    for j in range(4):
        across(j).wait_send()
        over(j).wait_send()
        share_near(j).wait_send()
        send_y(j).wait_send()
        for n in range(2):
            swap(n, j).wait_send()
    for k in range(3):
        send_a(k).wait_send()

    def drain(n, carry):
        for j in (1, 2, 3):
            give(n, j).wait_send()
            send_b(n, j).wait_send()
        return carry

    lax.fori_loop(0, 8, drain, 0)


def layer(features, values, weight, bias, cotangent, rows, picks, counts, pulls):
    dma = pltpu.SemaphoreType.DMA
    hbm = pl.BlockSpec(memory_space=pl.ANY)
    return pl.pallas_call(
        layer_kernel,
        name="layer",
        out_shape=(
            pltpu.VMEM((4, TILE, WIDTH), BF),
            pltpu.VMEM((4, TILE, WIDTH), F32),
            pltpu.VMEM((8, 32, WIDTH), F32),
            pltpu.VMEM((1, WIDTH), F32),
        ),
        in_specs=[hbm] * 9,
        out_specs=(pl.BlockSpec(memory_space=pltpu.VMEM),) * 4,
        scratch_shapes=[
            *[pltpu.VMEM((4, TILE, WIDTH), BF)] * 8,
            pltpu.VMEM((SECTIONS, SLOTS, TILE, TILE), BF),
            pltpu.VMEM((WIDTH, WIDTH), BF),
            pltpu.VMEM((1, WIDTH), F32),
            pltpu.VMEM((4, TILE, WIDTH), BF),
            pltpu.SMEM((SLOTS, SECTIONS), jnp.int32),
            pltpu.SMEM((SLOTS, SECTIONS), jnp.int32),
            pltpu.SMEM((1, SECTIONS), jnp.int32),
            pltpu.SMEM((2, SECTIONS), jnp.int32),
            pltpu.VMEM((2, SECTIONS), jnp.int32),
            pltpu.VMEM((3, 2, SECTIONS), jnp.int32),
            pltpu.SMEM((3, 2, SECTIONS), jnp.int32),
            pltpu.VMEM((3, 8, 2, TILE, WIDTH), BF),
            pltpu.VMEM((4, 8, 2, TILE, WIDTH), BF),
            pltpu.VMEM((129, TILE, WIDTH), F32),
            pltpu.SMEM((16,), jnp.int32),
            pltpu.VMEM((2, 4, TILE, WIDTH), F32),
            pltpu.VMEM((2, 4, TILE, WIDTH), F32),
            pltpu.VMEM((4, TILE, WIDTH), BF),
            pltpu.VMEM((4, TILE, WIDTH), BF),
            pltpu.VMEM((QUARTER, WIDTH), BF),
            pltpu.VMEM((QUARTER, WIDTH), BF),
            pltpu.VMEM((16, TILE, WIDTH), BF),
            pltpu.VMEM((4, 8, 2 * TILE, WIDTH), BF),
            pltpu.VMEM((3, 8, 2 * TILE, WIDTH), BF),
            pltpu.VMEM((4, 4, TILE, WIDTH), BF),
            pltpu.VMEM((4, 4, TILE, WIDTH), BF),
            pltpu.VMEM((4, 4, TILE, WIDTH), BF),
            pltpu.VMEM((3, 4, TILE, WIDTH), BF),
            pltpu.VMEM((8, 40, WIDTH), F32),
            pltpu.VMEM((8, 40, WIDTH), F32),
            pltpu.VMEM((4, 8, WIDTH), F32),
            pltpu.VMEM((4, 8, WIDTH), F32),
            pltpu.VMEM((8, WIDTH), F32),
            pltpu.VMEM((4, 8, WIDTH), F32),
            pltpu.VMEM((4, 8, WIDTH), F32),
            pltpu.VMEM((8, WIDTH), F32),
            pltpu.VMEM((4, 8, WIDTH), F32),
            pltpu.VMEM((8, WIDTH), F32),
            pltpu.VMEM((4, 8, WIDTH), F32),
            dma((8,)), *[dma] * 3, dma((3,)), dma((3,)),
            dma((3,)), dma((3,)), dma((2,)), dma((2,)), dma((4,)), dma((4,)), dma((3, 8)), dma((3, 8)),
            dma((2, 4)), dma((2, 4)), dma((4,)), dma((4,)),
            dma((4,)), dma((4,)), dma((4,)), dma((4,)), dma((4,)), dma((4,)),
            dma((3, 8)), dma((3, 8)), dma((4,)), dma((4,)), dma((3,)), dma((3,)),
            dma((7,)), dma((7,)), dma((3,)), dma((3,)), dma((3,)), dma((3,)),
            dma((3,)), dma((3,)), dma((7,)), dma((7,)),
            dma((3,)), dma((3,)), dma((3,)), dma((3,)),
        ],
        compiler_params=pltpu.CompilerParams(
            collective_id=1, has_side_effects=True, vmem_limit_bytes=VMEM_LIMIT
        ),
    )(
        features.reshape(16, TILE, WIDTH), values, weight, bias.reshape(1, WIDTH),
        cotangent.reshape(4, TILE, WIDTH), rows, picks, counts, pulls,
    )


def hand_over_kernel(*refs):
    sems = refs[8]
    copies = [pltpu.make_async_copy(refs[n], refs[4 + n], sems.at[n]) for n in range(4)]
    for copy in copies:
        copy.start()
    for copy in copies:
        copy.wait()


def hand_over(*arrays):
    hbm, vmem = pl.BlockSpec(memory_space=pl.ANY), pl.BlockSpec(memory_space=pltpu.VMEM)
    return pl.pallas_call(
        hand_over_kernel,
        name="hand_over",
        out_shape=tuple(jax.ShapeDtypeStruct(array.shape, array.dtype) for array in arrays),
        in_specs=[vmem] * 4,
        out_specs=(hbm,) * 4,
        scratch_shapes=[pltpu.SemaphoreType.DMA((4,))],
        compiler_params=pltpu.CompilerParams(vmem_limit_bytes=4 << 20),
    )(*arrays)


def local(
    features, weight, bias, cotangent, tile_vals, tile_rows, tile_pick, tile_count, pull_cols
):
    act, fgrad, wgrad, bgrad = hand_over(*layer(
        features,
        tile_vals.reshape(SECTIONS, SLOTS, TILE, TILE),
        weight,
        bias,
        cotangent,
        tile_rows.reshape(SECTIONS, SLOTS).T,
        tile_pick.reshape(SECTIONS, SLOTS).T,
        tile_count.reshape(1, SECTIONS),
        pull_cols.reshape(SECTIONS, 2).T,
    ))
    return (
        act.reshape(QUARTER, WIDTH),
        fgrad.reshape(QUARTER, WIDTH),
        wgrad.reshape(WIDTH, WIDTH),
        bgrad.reshape(WIDTH),
    )


def solution(mesh):
    in_specs = (
        P("rows", None),
        P(),
        P(),
        P(("rows", "rep"), None),
        P("rows", "rep", None, None, None, None),
        P("rows", "rep", None, None),
        P("rows", "rep", None, None),
        P("rows", "rep", None),
        P("rows", "rep", None, None),
    )
    out_specs = (P(("rows", "rep"), None), P(("rows", "rep"), None), P(), P())
    return jax.shard_map(local, mesh=mesh, in_specs=in_specs, out_specs=out_specs, check_vma=False)
```

```python
import functools

import jax
import jax.numpy as jnp
from jax import lax
from jax.experimental import pallas as pl
from jax.experimental.pallas import tpu as pltpu
from jax.sharding import PartitionSpec as P

MESH = pl.DeviceIdType.MESH
BF = jnp.bfloat16
F32 = jnp.float32
TILE = 128
WIDTH = 256
SECTIONS = 32
SLOTS = 4
QUARTER = 512
ROWS = 2048
VMEM_LIMIT = 60 << 20


class Place:
    def __init__(self):
        rows, rep = lax.axis_index("rows"), lax.axis_index("rep")
        self.yh, x, z = rows // 16, (rows // 4) % 4, rows % 4
        self.x, self.z = x, z
        self.yl, self.core = rep // 2, rep % 2
        self.a = x + self.core * (z - x)
        self.b = z + self.core * (x - z)

    def section(self, yh, a, b):
        x = a + self.core * (b - a)
        z = b + self.core * (a - b)
        return yh * 16 + x * 4 + z

    def a_peer(self, j):
        return (self.section(self.yh, (self.a + j) % 4, self.b), self.yl * 2 + self.core)

    def b_peer(self, j):
        return (self.section(self.yh, self.a, (self.b + j) % 4), self.yl * 2 + self.core)

    def y_peer(self):
        return (self.section(1 - self.yh, self.a, self.b), self.yl * 2 + self.core)

    def near_peer(self, mask):
        yh = (self.yh + mask // 4) % 2
        yl = (self.yl + (mask // 2) % 2) % 2
        core = (self.core + mask % 2) % 2
        rows = lax.axis_index("rows")
        return (yh * 16 + rows % 16, yl * 2 + core)

    def near_id(self):
        return self.yh * 4 + self.yl * 2 + self.core

    def x_peer(self, j):
        rows = lax.axis_index("rows")
        return (self.yh * 16 + (rows + 4 * j) % 16, self.yl * 2 + self.core)

    def z_peer(self, j):
        rows = lax.axis_index("rows")
        return (rows // 4 * 4 + (rows + j) % 4, self.yl * 2 + self.core)


def greet(peers):
    barrier = pltpu.get_barrier_semaphore()
    for peer in peers:
        pl.semaphore_signal(barrier, inc=1, device_id=peer, device_id_type=MESH)
    pl.semaphore_wait(barrier, len(peers))


def remote(src, dst, send, recv, peer):
    return pltpu.make_async_remote_copy(
        src_ref=src, dst_ref=dst, send_sem=send, recv_sem=recv, device_id=peer, device_id_type=MESH
    )


def masked(values, section, picks, counts):
    halves = []
    for p in range(2):
        parts = []
        for t in range(SLOTS):
            keep = jnp.logical_and(picks[t, section] == p, t < counts[0, section])
            scale = jnp.where(keep, jnp.float32(1), jnp.float32(0))
            parts.append(values[section, t] * jnp.full((TILE, TILE), scale, F32).astype(BF))
        halves.append(jnp.concatenate(parts, axis=0))
    return jnp.concatenate(halves, axis=1)


def layer_kernel(
    features, values_hbm, weight_hbm, bias_hbm, cot_hbm, rows_hbm, picks_hbm, counts_hbm, pulls_hbm,
    act, fgrad, wgrad, bgrad, *scratch,
):
    dense, scratch = scratch[:8], scratch[8:]
    (values, weight, bias, cotangent, rows, picks, counts, pulls, pull_vec, asked, wants, packed, got, running, last,
     swap_out, from_core, to_near, from_near, agg_all, slope_all, back,
     terms, from_b, to_y, from_y, to_a, from_a,
     w0, n1, s1, w2, s2, w3, s4, b1, x1, b2, z1,
     load_sem, own_sem, pull_sem, want_sem, ask_send, ask_recv,
     fa_send, fa_recv, fr_send, fr_recv, fy_send, fy_recv, fb_send, fb_recv,
     core_send, core_recv, near_send, near_recv,
     gc_send, gc_recv, gn_send, gn_recv, gf_send, gf_recv,
     b_send, b_recv, y_send, y_recv, a_send, a_recv,
     n1_send, n1_recv, w2_send, w2_recv, w3_send, w3_recv, w4_send, w4_recv, w5_send, w5_recv,
     x1_send, x1_recv, z1_send, z1_recv) = scratch
    me = Place()
    fetch = pltpu.make_async_copy(
        features.at[pl.ds((me.yl * 2 + me.core) * 4, 4)], dense[0], own_sem
    )
    fetch.start()
    fetch_pull = pltpu.make_async_copy(pulls_hbm, pull_vec, pull_sem)
    fetch_pull.start()
    loads = [
        pltpu.make_async_copy(src, dst, load_sem.at[n])
        for n, (src, dst) in enumerate([
            (pulls_hbm, pulls), (rows_hbm, rows), (picks_hbm, picks), (counts_hbm, counts),
            (values_hbm, values), (weight_hbm, weight), (bias_hbm, bias), (cot_hbm, cotangent),
        ])
    ]
    for load in loads:
        load.start()
    greet(
        [me.near_peer(m) for m in range(1, 8)]
        + [me.a_peer(j) for j in (1, 2, 3)]
        + [me.b_peer(j) for j in (1, 2, 3)]
    )

    def ask(j):
        return remote(pull_vec, asked.at[j - 1], ask_send.at[j - 1], ask_recv.at[j - 1], me.b_peer(j))

    fetch_pull.wait()
    for j in (1, 2, 3):
        ask(j).start()
    fetch.wait()

    def along(j):
        return remote(dense[0], dense[j], fa_send.at[j - 1], fa_recv.at[j - 1], me.a_peer(j))

    def relay(j):
        half = pl.ds(j // 2 * 2, 2)
        return remote(
            dense[j].at[half], dense[2].at[half], fr_send.at[j // 2], fr_recv.at[j // 2], me.a_peer(j)
        )

    def across(j):
        return remote(dense[j], dense[4 + j], fy_send.at[j], fy_recv.at[j], me.y_peer())

    def give(n, to):
        return remote(
            packed.at[to - 1, n], got.at[to, n], fb_send.at[to - 1, n], fb_recv.at[to - 1, n], me.b_peer(to)
        )

    def block_section(n, b):
        return me.section((me.yh + n // 4) % 2, (me.a + 4 - n % 4) % 4, b)

    for j in (1, 3):
        along(j).start()
    across(0).start()
    loads[0].wait()
    for j in (1, 2, 3):
        ask(j).wait()
        table = pltpu.make_async_copy(asked.at[j - 1], wants.at[j - 1], want_sem)
        table.start()
        table.wait()

    def serve(n):
        column = block_section(n, me.b)
        for source in (1, 3, 2):
            to = 4 - source
            for p in range(2):
                packed[to - 1, n, p] = dense[n][wants[source - 1, p, column]]
            give(n, to).start()
        for p in range(2):
            got[0, n, p] = dense[n][pulls[p, column]]

    serve(0)
    for j in (1, 3):
        along(j).wait_recv()
        relay(j).start()
        across(j).start()
        serve(j)
    for j in (1, 3):
        relay(j).wait_recv()
    across(2).start()
    serve(2)
    for j in (0, 1, 3, 2):
        across(j).wait_recv()
        serve(4 + j)

    for load in loads[1:]:
        load.wait()
    running[128] = jnp.zeros((TILE, WIDTH), F32)

    def forward(step, carry):
        ends = list(carry)
        n = step // 4 * 4 + (step % 4 + (step % 4) // 2 * (5 - 2 * (step % 4)))
        for j in (1, 2, 3):
            give(n, j).wait_recv()
        for source in range(4):
            section = block_section(n, (me.b + 4 - source) % 4)
            block = got[source, n].reshape(2 * TILE, WIDTH)
            sums = jnp.dot(masked(values, section, picks, counts), block, preferred_element_type=F32)
            for t in range(SLOTS):
                row = rows[t, section]
                before = jnp.int32(128)
                slot = (step * 4 + source) * 4 + t
                for r in range(16):
                    before = jnp.where(row == r, ends[r], before)
                    ends[r] = jnp.where(row == r, slot, ends[r])
                running[slot] = sums[t * TILE:(t + 1) * TILE] + running[before]
        return tuple(ends)

    ends = lax.fori_loop(0, 8, forward, (jnp.int32(128),) * 16)
    for r in range(16):
        last[r] = ends[r]

    def part(r):
        return running[last[r]]

    core_peer, near_peer = me.near_peer(1), me.near_peer(2)
    quarters = [(1 - me.yl) * 2, me.yl * 2]

    def swap(n, t):
        return remote(swap_out.at[n, t], from_core.at[n, t], core_send.at[n, t], core_recv.at[n, t], core_peer)

    def over(t):
        return remote(to_near.at[t], from_near.at[t], near_send.at[t], near_recv.at[t], near_peer)

    for n in range(2):
        for t in range(4):
            swap_out[n, t] = part((quarters[n] + 1 - me.core) * 4 + t)
            swap(n, t).start()
    for t in range(4):
        swap(0, t).wait_recv()
        to_near[t] = (part((quarters[0] + me.core) * 4 + t) + from_core[0, t]).astype(BF)
        over(t).start()

    mine = me.yl * 2 + me.core
    yours = (1 - me.yl) * 2 + me.core

    def share_core(t):
        ref = back.at[mine * 4 + t]
        return remote(ref, ref, gc_send.at[t], gc_recv.at[t], core_peer)

    def share_near(t):
        ref = back.at[mine * 4 + t]
        return remote(ref, ref, gn_send.at[t], gn_recv.at[t], near_peer)

    def forward_on(t):
        ref = back.at[yours * 4 + t]
        return remote(ref, ref, gf_send.at[t], gf_recv.at[t], core_peer)

    for t in range(4):
        swap(1, t).wait_recv()
        over(t).wait_recv()
        agg = (part(mine * 4 + t) + from_core[1, t] + from_near[t].astype(F32)).astype(BF)
        agg_all[t * TILE:(t + 1) * TILE] = agg
        pre = jnp.dot(agg, weight[...], preferred_element_type=F32) + bias[...]
        sig = 1.0 / (1.0 + jnp.exp(-pre))
        act[t] = (pre * sig).astype(BF)
        slope = (cotangent[t].astype(F32) * (sig * (1.0 + pre * (1.0 - sig)))).astype(BF)
        slope_all[t * TILE:(t + 1) * TILE] = slope
        back[mine * 4 + t] = lax.dot_general(
            slope, weight[...], (((1,), (1,)), ((), ())), preferred_element_type=F32
        ).astype(BF)
        share_near(t).start()
        share_core(t).start()

    grad = lax.dot_general(
        agg_all[...], slope_all[...], (((0,), (0,)), ((), ())), preferred_element_type=F32
    )
    bias_sum = jnp.sum(slope_all[...].astype(F32), axis=0, keepdims=True)
    for m in range(8):
        w0[m, :32] = grad[m * 32:(m + 1) * 32]
        w0[m, 32:40] = jnp.broadcast_to(bias_sum, (8, WIDTH))

    def n1_copy(m):
        other = (me.yh + m // 4) % 2 * 4 + (me.yl + m // 2 % 2) % 2 * 2 + (me.core + m % 2) % 2
        return remote(
            w0.at[other], n1.at[me.near_id()], n1_send.at[m - 1], n1_recv.at[m - 1], me.near_peer(m)
        )

    def w2_copy(j):
        return remote(
            s1.at[(me.a + j) % 4], w2.at[me.a], w2_send.at[j - 1], w2_recv.at[j - 1], me.a_peer(j)
        )

    def x1_copy(j):
        return remote(b1, x1.at[me.x], x1_send.at[j - 1], x1_recv.at[j - 1], me.x_peer(j))

    def w3_copy(j):
        return remote(s2, w3.at[me.b], w3_send.at[j - 1], w3_recv.at[j - 1], me.b_peer(j))

    def z1_copy(j):
        return remote(b2, z1.at[me.z], z1_send.at[j - 1], z1_recv.at[j - 1], me.z_peer(j))

    def w4_copy(j):
        return remote(s4.at[me.a], s4.at[me.a], w4_send.at[j - 1], w4_recv.at[j - 1], me.a_peer(j))

    def w5_copy(m):
        ref = wgrad.at[me.near_id()]
        return remote(ref, ref, w5_send.at[m - 1], w5_recv.at[m - 1], me.near_peer(m))

    for m in range(1, 8):
        n1_copy(m).start()
    n1[me.near_id()] = w0[me.near_id()]

    def weight_over_a():
        for m in range(1, 8):
            n1_copy(m).wait()
        total = n1[0]
        for m in range(1, 8):
            total = total + n1[m]
        for a in range(4):
            s1[a] = total[a * 8:(a + 1) * 8]
        b1[...] = total[32:40]
        for j in (1, 2, 3):
            w2_copy(j).start()
            x1_copy(j).start()
        w2[me.a] = s1[me.a]
        x1[me.x] = b1[...]

    def weight_over_b():
        for j in (1, 2, 3):
            w2_copy(j).wait()
            x1_copy(j).wait()
        s2[...] = w2[0] + w2[1] + w2[2] + w2[3]
        b2[...] = x1[0] + x1[1] + x1[2] + x1[3]
        for j in (1, 2, 3):
            w3_copy(j).start()
            z1_copy(j).start()
        w3[me.b] = s2[...]
        z1[me.z] = b2[...]

    def weight_back_a():
        for j in (1, 2, 3):
            w3_copy(j).wait()
            z1_copy(j).wait()
        s4[me.a] = w3[0] + w3[1] + w3[2] + w3[3]
        bgrad[...] = (z1[0] + z1[1] + z1[2] + z1[3])[:1]
        for j in (1, 2, 3):
            w4_copy(j).start()

    def weight_back_near():
        for j in (1, 2, 3):
            w4_copy(j).wait()
        wgrad[me.near_id()] = s4[...].reshape(32, WIDTH)
        for m in range(1, 8):
            w5_copy(m).start()

    for t in range(4):
        share_near(t).wait_recv()
        forward_on(t).start()
    for t in range(4):
        share_core(t).wait()
        forward_on(t).wait()

    def step_a(k):
        return 2 - k + k // 2 * 3 - k // 3 * 2

    def place(k):
        return (me.yh + 1 + k // 4) % 2, (me.a + step_a(k % 4)) % 4

    def send_b(k, j):
        return remote(
            terms.at[j, k], from_b.at[j - 1, k], b_send.at[j - 1, k], b_recv.at[j - 1, k], me.b_peer(j)
        )

    def products(k, j):
        yh, a = place(k)
        section = me.section(yh, a, (me.b + j) % 4)
        sources = jnp.concatenate([back[rows[t, section]] for t in range(SLOTS)], axis=0)
        terms[j, k] = lax.dot_general(
            masked(values, section, picks, counts), sources, (((0,), (0,)), ((), ())),
            preferred_element_type=F32,
        ).astype(BF)

    def contribute(k):
        for j in (1, 3, 2):
            products(k, j)
            send_b(k, j).start()

    def send_y(k):
        return remote(to_y.at[k], from_y.at[k], y_send.at[k], y_recv.at[k], me.y_peer())

    def send_a(k):
        return remote(to_a.at[k], from_a.at[k], a_send.at[k], a_recv.at[k], me.a_peer(step_a(k)))

    def gather_b(k, q):
        yh, a = place(k)
        section = me.section(yh, a, me.b)
        sums = jnp.zeros((TILE, WIDTH), F32)
        for source in range(4):
            for p in range(2):
                if source == 0:
                    hit, tile = pulls[p, section] == q, terms[0, k, p * TILE:(p + 1) * TILE]
                else:
                    hit = wants[source - 1, p, section] == q
                    tile = from_b[source - 1, k, p * TILE:(p + 1) * TILE]
                sums += tile.astype(F32) * jnp.where(hit, jnp.float32(1), jnp.float32(0))
        return sums

    def arrive_b(k):
        for j in (1, 2, 3):
            send_b(k, j).wait_recv()

    def start(k, carry):
        contribute(k)
        pl.when(k == 2)(weight_over_a)
        return carry

    def other_half(k, carry):
        @pl.when(k + 3 < 8)
        def _():
            contribute(3 + k)

        products(k, 0)
        arrive_b(k)

        def column(q, inner):
            to_y[k, q] = gather_b(k, q).astype(BF)
            return inner

        lax.fori_loop(0, 4, column, 0)
        send_y(k).start()
        pl.when(k == 0)(weight_over_b)
        pl.when(k == 2)(weight_back_a)
        return carry

    def this_half(k, carry):
        @pl.when(k + 4 + 3 < 8)
        def _():
            contribute(4 + 3 + k)

        products(4 + k, 0)
        arrive_b(4 + k)
        send_y(k).wait_recv()

        def column(q, inner):
            to_a[k, q] = (gather_b(4 + k, q) + from_y[k, q].astype(F32)).astype(BF)
            return inner

        lax.fori_loop(0, 4, column, 0)
        send_a(k).start()
        pl.when(k == 0)(weight_back_near)
        return carry

    lax.fori_loop(0, 3, start, 0)
    lax.fori_loop(0, 4, other_half, 0)
    lax.fori_loop(0, 3, this_half, 0)
    products(7, 0)
    arrive_b(7)
    send_y(3).wait_recv()
    for k in range(3):
        send_a(k).wait_recv()

    def own(q, carry):
        fgrad[q] = gather_b(7, q) + sum(
            (ref[n, q].astype(F32) for ref, n in ((from_y, 3), (from_a, 0), (from_a, 1), (from_a, 2))),
            jnp.zeros((TILE, WIDTH), F32),
        )
        return carry

    lax.fori_loop(0, 4, own, 0)
    for m in range(1, 8):
        w5_copy(m).wait()

    for j in (1, 3):
        along(j).wait_send()
        relay(j).wait_send()
    for j in range(4):
        across(j).wait_send()
        over(j).wait_send()
        share_near(j).wait_send()
        send_y(j).wait_send()
        for n in range(2):
            swap(n, j).wait_send()
    for k in range(3):
        send_a(k).wait_send()

    def drain(n, carry):
        for j in (1, 2, 3):
            give(n, j).wait_send()
            send_b(n, j).wait_send()
        return carry

    lax.fori_loop(0, 8, drain, 0)


def layer(features, values, weight, bias, cotangent, rows, picks, counts, pulls):
    dma = pltpu.SemaphoreType.DMA
    hbm = pl.BlockSpec(memory_space=pl.ANY)
    return pl.pallas_call(
        layer_kernel,
        name="layer",
        out_shape=(
            pltpu.VMEM((4, TILE, WIDTH), BF),
            pltpu.VMEM((4, TILE, WIDTH), F32),
            pltpu.VMEM((8, 32, WIDTH), F32),
            pltpu.VMEM((1, WIDTH), F32),
        ),
        in_specs=[hbm] * 9,
        out_specs=(pl.BlockSpec(memory_space=pltpu.VMEM),) * 4,
        scratch_shapes=[
            *[pltpu.VMEM((4, TILE, WIDTH), BF)] * 8,
            pltpu.VMEM((SECTIONS, SLOTS, TILE, TILE), BF),
            pltpu.VMEM((WIDTH, WIDTH), BF),
            pltpu.VMEM((1, WIDTH), F32),
            pltpu.VMEM((4, TILE, WIDTH), BF),
            pltpu.SMEM((SLOTS, SECTIONS), jnp.int32),
            pltpu.SMEM((SLOTS, SECTIONS), jnp.int32),
            pltpu.SMEM((1, SECTIONS), jnp.int32),
            pltpu.SMEM((2, SECTIONS), jnp.int32),
            pltpu.VMEM((2, SECTIONS), jnp.int32),
            pltpu.VMEM((3, 2, SECTIONS), jnp.int32),
            pltpu.SMEM((3, 2, SECTIONS), jnp.int32),
            pltpu.VMEM((3, 8, 2, TILE, WIDTH), BF),
            pltpu.VMEM((4, 8, 2, TILE, WIDTH), BF),
            pltpu.VMEM((129, TILE, WIDTH), F32),
            pltpu.SMEM((16,), jnp.int32),
            pltpu.VMEM((2, 4, TILE, WIDTH), F32),
            pltpu.VMEM((2, 4, TILE, WIDTH), F32),
            pltpu.VMEM((4, TILE, WIDTH), BF),
            pltpu.VMEM((4, TILE, WIDTH), BF),
            pltpu.VMEM((QUARTER, WIDTH), BF),
            pltpu.VMEM((QUARTER, WIDTH), BF),
            pltpu.VMEM((16, TILE, WIDTH), BF),
            pltpu.VMEM((4, 8, 2 * TILE, WIDTH), BF),
            pltpu.VMEM((3, 8, 2 * TILE, WIDTH), BF),
            pltpu.VMEM((4, 4, TILE, WIDTH), BF),
            pltpu.VMEM((4, 4, TILE, WIDTH), BF),
            pltpu.VMEM((4, 4, TILE, WIDTH), BF),
            pltpu.VMEM((3, 4, TILE, WIDTH), BF),
            pltpu.VMEM((8, 40, WIDTH), F32),
            pltpu.VMEM((8, 40, WIDTH), F32),
            pltpu.VMEM((4, 8, WIDTH), F32),
            pltpu.VMEM((4, 8, WIDTH), F32),
            pltpu.VMEM((8, WIDTH), F32),
            pltpu.VMEM((4, 8, WIDTH), F32),
            pltpu.VMEM((4, 8, WIDTH), F32),
            pltpu.VMEM((8, WIDTH), F32),
            pltpu.VMEM((4, 8, WIDTH), F32),
            pltpu.VMEM((8, WIDTH), F32),
            pltpu.VMEM((4, 8, WIDTH), F32),
            dma((8,)), *[dma] * 3, dma((3,)), dma((3,)),
            dma((3,)), dma((3,)), dma((2,)), dma((2,)), dma((4,)), dma((4,)), dma((3, 8)), dma((3, 8)),
            dma((2, 4)), dma((2, 4)), dma((4,)), dma((4,)),
            dma((4,)), dma((4,)), dma((4,)), dma((4,)), dma((4,)), dma((4,)),
            dma((3, 8)), dma((3, 8)), dma((4,)), dma((4,)), dma((3,)), dma((3,)),
            dma((7,)), dma((7,)), dma((3,)), dma((3,)), dma((3,)), dma((3,)),
            dma((3,)), dma((3,)), dma((7,)), dma((7,)),
            dma((3,)), dma((3,)), dma((3,)), dma((3,)),
        ],
        compiler_params=pltpu.CompilerParams(
            collective_id=1, has_side_effects=True, vmem_limit_bytes=VMEM_LIMIT
        ),
    )(
        features.reshape(16, TILE, WIDTH), values, weight, bias.reshape(1, WIDTH),
        cotangent.reshape(4, TILE, WIDTH), rows, picks, counts, pulls,
    )


def hand_over_kernel(*refs):
    sems = refs[8]
    copies = [pltpu.make_async_copy(refs[n], refs[4 + n], sems.at[n]) for n in range(4)]
    for copy in copies:
        copy.start()
    for copy in copies:
        copy.wait()


def hand_over(*arrays):
    hbm, vmem = pl.BlockSpec(memory_space=pl.ANY), pl.BlockSpec(memory_space=pltpu.VMEM)
    return pl.pallas_call(
        hand_over_kernel,
        name="hand_over",
        out_shape=tuple(jax.ShapeDtypeStruct(array.shape, array.dtype) for array in arrays),
        in_specs=[vmem] * 4,
        out_specs=(hbm,) * 4,
        scratch_shapes=[pltpu.SemaphoreType.DMA((4,))],
        compiler_params=pltpu.CompilerParams(vmem_limit_bytes=4 << 20),
    )(*arrays)


def local(
    features, weight, bias, cotangent, tile_vals, tile_rows, tile_pick, tile_count, pull_cols
):
    act, fgrad, wgrad, bgrad = hand_over(*layer(
        features,
        tile_vals.reshape(SECTIONS, SLOTS, TILE, TILE),
        weight,
        bias,
        cotangent,
        tile_rows.reshape(SECTIONS, SLOTS).T,
        tile_pick.reshape(SECTIONS, SLOTS).T,
        tile_count.reshape(1, SECTIONS),
        pull_cols.reshape(SECTIONS, 2).T,
    ))
    return (
        act.reshape(QUARTER, WIDTH),
        fgrad.reshape(QUARTER, WIDTH),
        wgrad.reshape(WIDTH, WIDTH),
        bgrad.reshape(WIDTH),
    )


def solution(mesh):
    in_specs = (
        P("rows", None),
        P(),
        P(),
        P(("rows", "rep"), None),
        P("rows", "rep", None, None, None, None),
        P("rows", "rep", None, None),
        P("rows", "rep", None, None),
        P("rows", "rep", None),
        P("rows", "rep", None, None),
    )
    out_specs = (P(("rows", "rep"), None), P(("rows", "rep"), None), P(), P())
    return jax.shard_map(local, mesh=mesh, in_specs=in_specs, out_specs=out_specs, check_vma=False)
```
